512 devices in a mesh: seq: 32 (over x, z), batch: 16 (over y, core).
Axes of the slice: x: 4, y: 8, z: 8, core: 2. Of those that a mesh axis runs over, the one named last changes fastest.
Arguments:
- feats: bfloat16 [16, 16384, 512], P('batch', 'seq'), may hold values from -16 to 16
- hilbert_pos: int32 [16, 16384], P('batch', 'seq'), may hold values from 0 to 16383, as said below
- w_qkv: bfloat16 [512, 1536], P('seq'), may hold values from -2 to 2
- w_out: bfloat16 [512, 512], P('seq'), may hold values from -0.25 to 0.25
- grad_out: bfloat16 [16, 16384, 512], P('batch', 'seq'), may hold values from -6 to 6
Outputs:
- mixed_out: bfloat16 [16, 16384, 512], P('batch', 'seq')
- feat_grad: bfloat16 [16, 16384, 512], P('batch', 'seq')
- qkv_wgrad: float32 [512, 1536], P('seq')
- out_wgrad: float32 [512, 512], P('seq')
The draws below stay inside these ranges and needn't reach their ends.
Inputs may be any that keep to these rules, and one draw needn't show every extreme that they name: `hilbert_pos`: each tile's row is a permutation of the tile's points. Of the 512 points of one aligned block (the points of one index of seq), at most 32 have positions in any one aligned block; every block keeps exactly 32 of its own points, and every block of a tile sends the same list of counts to the blocks 1, 2, ... places after it (cyclically).
All inputs are finite; a program needn't handle non-finite values.
Results may differ from the reference program's by a relative error of at most 0.034.
The reference program's roundings to bfloat16 on the way count: a program that leaves them out, or rounds other values in their place, can miss the bound.
Values may be sent and summed in bfloat16 or wider, within the bound.
No kernel may reach another device: no remote copies, remote signals or barrier semaphores. Data moves between devices by JAX's collectives and lax.ppermute only.
A program may use at most 64 MiB of HBM per device.

```python
import jax
import jax.numpy as jnp
from jax import lax

WIDTH = 512
HEADS = 32
HEAD_CHANNELS = 16
PATCH = 128
P_DEV = 512
CAP = 32
TILES = 16
NPTS = 16384
N_SEQ = 32


def curve_table(key):

    def one_tile(tile_key):
        first_key, second_key, third_key, fourth_key = jax.random.split(tile_key, 4)
        remain = P_DEV - CAP
        others = N_SEQ - 1
        level = remain // others
        excess = remain - level * others
        counts = level + (jnp.arange(others) < excess).astype(jnp.int32)
        paired = others // 2
        spread = min(level, CAP - level - 1)
        delta = jax.random.randint(first_key, (paired,), -spread, spread + 1)
        evens = 2 * jnp.arange(paired)
        counts = counts.at[evens].add(delta).at[evens + 1].add(-delta)
        counts = jax.random.permutation(second_key, counts)
        sizes = jnp.concatenate([jnp.array([CAP], jnp.int32), counts.astype(jnp.int32)])
        starts = jnp.cumsum(sizes) - sizes
        local_slot = jnp.arange(P_DEV)
        offset_of = jnp.sum((local_slot[:, None] >= starts[None, 1:]).astype(jnp.int32), axis=1)
        devices = jnp.arange(N_SEQ)
        target_dev = (devices[:, None] + offset_of[None, :]) % N_SEQ
        arrival = jax.vmap(lambda sub_key: jax.random.permutation(sub_key, P_DEV))(jax.random.split(third_key, N_SEQ))
        landing = target_dev * P_DEV + arrival[target_dev, local_slot[None, :]]
        leaving = jax.vmap(lambda sub_key: jax.random.permutation(sub_key, P_DEV))(jax.random.split(fourth_key, N_SEQ))
        curve_pos = jnp.zeros((N_SEQ, P_DEV), jnp.int32).at[devices[:, None], leaving].set(landing.astype(jnp.int32))
        return curve_pos.reshape(NPTS)
    return jax.vmap(one_tile)(jax.random.split(key, TILES))


def draw_hilbert_pos(key, part):
    return curve_table(key)


def draw_feats(key, part):
    key = jax.random.fold_in(key, 5)
    first_key = jax.random.fold_in(key, 0)
    value_matrix = jnp.clip(jax.random.normal(first_key, (TILES, NPTS, WIDTH), jnp.float32), -6.0, 6.0)
    return value_matrix.astype(jnp.bfloat16)


def draw_w_qkv(key, part):
    key = jax.random.fold_in(key, 7)
    first_key = jax.random.fold_in(key, 0)
    value_matrix = jnp.clip(jax.random.normal(first_key, (WIDTH, 3 * WIDTH), jnp.float32), -6.0, 6.0) * WIDTH ** (-0.5)
    return value_matrix.astype(jnp.bfloat16)


def level_of(own_key, dims, cuts, least, largest):
    level = 1.0
    for axis_at, shards_of in cuts:
        draws = jax.random.uniform(jax.random.fold_in(jax.random.fold_in(own_key, 6), axis_at), (shards_of,), jnp.float32, least / len(cuts), largest / len(cuts))
        level = level * jnp.repeat(jnp.exp(draws), dims[axis_at] // shards_of).reshape((-1,) + (1,) * (len(dims) - 1 - axis_at))
    return level


def normal_values(own_key, dims, width, limit, cuts=(), held_as=jnp.bfloat16):
    values = jax.random.normal(own_key, dims, jnp.float32) * width
    if len(cuts) > 0:
        values = level_of(own_key, dims, cuts, -0.22, 0.18) * values
    return jnp.clip(values, min=-limit, max=limit).astype(held_as)


def setup_inputs(seed: int = 0) -> dict:
    splits = jax.random.split(jax.random.key(seed), 6)
    return {
        "feats": draw_feats(jax.random.fold_in(splits[5], 71), 0),
        "hilbert_pos": draw_hilbert_pos(jax.random.fold_in(splits[5], 71), 0),
        "w_qkv": draw_w_qkv(jax.random.fold_in(splits[5], 71), 0),
        "w_out": normal_values(splits[3], (WIDTH, WIDTH), WIDTH ** -0.5, 0.25, ((0, 32),)),
        "grad_out": normal_values(splits[4], (TILES, NPTS, WIDTH), 1.0, 6.0, ((0, 16), (1, 32))),
    }


eps = 1e-05

def rounded_result(value_matrix):
    return lax.optimization_barrier(value_matrix.astype(jnp.bfloat16)).astype(jnp.float32)

def layer_norm(tile_rows):
    row_mean = lax.optimization_barrier(jnp.mean(tile_rows, axis=-1, keepdims=True))
    centred = tile_rows - row_mean
    spread = lax.optimization_barrier(jnp.mean(centred * centred, axis=-1, keepdims=True))
    inv_scale = lax.rsqrt(spread + eps)
    return (centred * inv_scale, inv_scale)

def split_heads(matrix):
    return matrix.reshape(matrix.shape[0], HEADS, HEAD_CHANNELS).transpose(1, 0, 2)

def merge_heads(stacked):
    return stacked.transpose(1, 0, 2).reshape(stacked.shape[1], WIDTH)

def patch_probs(qkv_rows):
    query_matrix = split_heads(qkv_rows[:, :WIDTH])
    key_matrix = split_heads(qkv_rows[:, WIDTH:2 * WIDTH])
    value_matrix = split_heads(qkv_rows[:, 2 * WIDTH:])
    score_matrix = jnp.einsum('kja,kea->kje', query_matrix, key_matrix) * HEAD_CHANNELS ** (-0.5)
    return (query_matrix, key_matrix, value_matrix, jax.nn.softmax(score_matrix, axis=-1))

def patch_forward(qkv_rows):
    query_matrix, key_matrix, value_matrix, probability_table = patch_probs(qkv_rows)
    context_rows = rounded_result(jnp.einsum('rno,rof->rnf', rounded_result(probability_table), value_matrix))
    return merge_heads(context_rows)

def patch_backward(operands):
    qkv_rows, ctx_grad = operands
    query_matrix, key_matrix, value_matrix, probability_table = patch_probs(qkv_rows)
    incoming_gradient = split_heads(ctx_grad)
    value_gradient = rounded_result(jnp.einsum('srw,srg->swg', rounded_result(probability_table), incoming_gradient))
    probability_gradient = jnp.einsum('kja,kea->kje', incoming_gradient, value_matrix)
    score_gradient = rounded_result(probability_table * (probability_gradient - lax.optimization_barrier(jnp.sum(probability_table * probability_gradient, axis=-1, keepdims=True))) * HEAD_CHANNELS ** (-0.5))
    query_gradient = rounded_result(jnp.einsum('rno,rof->rnf', score_gradient, key_matrix))
    key_gradient = rounded_result(jnp.einsum('srw,srg->swg', score_gradient, query_matrix))
    return jnp.concatenate([merge_heads(query_gradient), merge_heads(key_gradient), merge_heads(value_gradient)], axis=1)

def reference(feats, hilbert_pos, w_qkv, w_out, grad_out):
    factor = (TILES * NPTS) ** (-0.5)
    patches = NPTS // PATCH

    def one_tile(totals, tile_data):
        tile_rows, target, incoming_gradient = tile_data
        hilbert = jnp.zeros((NPTS, WIDTH), jnp.float32).at[target].set(tile_rows.astype(jnp.float32))
        normal_rows, inv_scale = layer_norm(hilbert)
        normed = normal_rows.astype(jnp.bfloat16)
        qkv_rows = jnp.dot(normed, w_qkv, preferred_element_type=jnp.float32).astype(jnp.bfloat16)
        qkv_patches = qkv_rows.astype(jnp.float32).reshape(patches, PATCH, 3 * WIDTH)
        context_rows = lax.map(patch_forward, qkv_patches).reshape(NPTS, WIDTH).astype(jnp.bfloat16)
        mixed_out = (hilbert + jnp.dot(context_rows, w_out, preferred_element_type=jnp.float32)).astype(jnp.bfloat16)
        ctx_grad = jnp.dot(incoming_gradient, w_out.T, preferred_element_type=jnp.float32).astype(jnp.bfloat16)
        grad_patches = ctx_grad.astype(jnp.float32).reshape(patches, PATCH, WIDTH)
        qkv_grad = lax.map(patch_backward, (qkv_patches, grad_patches)).reshape(NPTS, 3 * WIDTH).astype(jnp.bfloat16)
        term_qkv = jnp.dot(normed.T, qkv_grad, preferred_element_type=jnp.float32) * factor
        term_out = jnp.dot(context_rows.T, incoming_gradient, preferred_element_type=jnp.float32) * factor
        normed_grad = jnp.dot(qkv_grad, w_qkv.T, preferred_element_type=jnp.float32)
        centre_grad = normed_grad - lax.optimization_barrier(jnp.mean(normed_grad, axis=-1, keepdims=True))
        centre_grad = centre_grad - normal_rows * lax.optimization_barrier(jnp.mean(normed_grad * normal_rows, axis=-1, keepdims=True))
        hilbert_grad = (incoming_gradient.astype(jnp.float32) + inv_scale * centre_grad).astype(jnp.bfloat16)
        feat_grad = hilbert_grad[target]
        return ((totals[0] + term_qkv, totals[1] + term_out), (mixed_out, feat_grad))
    start = (jnp.zeros((WIDTH, 3 * WIDTH), jnp.float32), jnp.zeros((WIDTH, WIDTH), jnp.float32))
    totals, outputs = lax.scan(one_tile, start, (feats, hilbert_pos, grad_out))
    return (outputs[0], outputs[1], totals[0], totals[1])
```

```python
import functools
import math

import jax
import jax.numpy as jnp
from jax import lax
from jax.experimental import pallas as pl
from jax.experimental.pallas import tpu as pltpu
from jax.sharding import Mesh
from jax.sharding import PartitionSpec as P

HEADS = 32
HEAD_CHANNELS = 16
PATCH = 128
WIDTH = 512
POINTS = 512
SHARDS = 32
CAP = 32
SLOTS = SHARDS * CAP
LANES = 128
EPS = 1e-05
SCALE = HEAD_CHANNELS ** (-0.5)

BF = jnp.bfloat16
F32 = jnp.float32
SEQ = ("x", "z")
BATCH = ("y", "core")

FEAT_ROWS = 4 * CAP
POS_ROWS = CAP
W_ROWS = 8 * 16
SEND_ROWS = FEAT_ROWS + POS_ROWS + W_ROWS


def iota(shape, dim):
    return lax.broadcasted_iota(jnp.int32, shape, dim)


def onehot(condition):
    return jnp.where(condition, 1.0, 0.0).astype(BF)


def dot(left, right):
    return jnp.dot(left, right, preferred_element_type=F32)


def dot_t(left, right):
    return lax.dot_general(left, right, (((1,), (1,)), ((), ())), preferred_element_type=F32)


def pack_kernel(core_ref, pos_ref, feats_ref, wqkv_ref, wout_ref, out_ref, slot_ref):
    group = core_ref[0]
    target = pos_ref[...]
    owner = target // POINTS
    place = target % POINTS + 1
    mine = iota((SHARDS, POINTS), 0) == owner
    before = onehot(iota((POINTS, POINTS), 0) < iota((POINTS, POINTS), 1))
    ranks = dot(onehot(mine), before)
    rank = jnp.sum(jnp.where(mine, ranks, 0.0), axis=0, keepdims=True).astype(jnp.int32)
    slot = owner * CAP + rank
    slot_ref[...] = jnp.broadcast_to(slot, slot_ref.shape)
    place_of = onehot(iota((SLOTS, POINTS), 0) == slot)
    row = iota((LANES, POINTS), 0)
    digits = jnp.where(row == 0, place // 32, jnp.where(row == 1, place % 32, 0))
    pos = dot_t(place_of, digits.astype(F32).astype(BF)).astype(BF)
    out_ref[:, FEAT_ROWS : FEAT_ROWS + POS_ROWS, :] = pos.reshape(SHARDS, CAP, LANES)
    for c in range(4):
        rows = dot(place_of, feats_ref[:, c * LANES : (c + 1) * LANES]).astype(BF)
        out_ref[:, c * CAP : (c + 1) * CAP, :] = rows.reshape(SHARDS, CAP, LANES)
    base = FEAT_ROWS + POS_ROWS
    for part in range(4):
        for b in range(2):
            at = (2 * part + b) * 16
            lanes = pl.ds(pl.multiple_of(group * 256 + b * LANES, LANES), LANES)
            if part < 3:
                lanes = pl.ds(pl.multiple_of(group * 256 + part * WIDTH + b * LANES, LANES), LANES)
                piece = wqkv_ref[:, lanes]
            else:
                piece = wout_ref[:, lanes]
            out_ref[:, base + at : base + at + 16, :] = jnp.broadcast_to(
                piece[None], (SHARDS, 16, LANES)
            )


def main_kernel(
    core_ref,
    recv_ref,
    other_ref,
    gout_ref,
    mixed_ref,
    back_ref,
    keep_ref,
    send_ref,
    wqkv,
    wout,
    hil,
    nrm,
    qkv,
    cgrad,
    ctx_t,
    qg_t,
):
    group = core_ref[0]
    for part in range(4):
        for b in range(2):
            at = (2 * part + b) * 16
            mine = recv_ref[:, FEAT_ROWS + POS_ROWS + at : FEAT_ROWS + POS_ROWS + at + 16, :]
            theirs = other_ref[:, at : at + 16, :]
            for piece, g in ((mine, group), (theirs, 1 - group)):
                piece = piece.reshape(WIDTH, LANES)
                if part < 3:
                    wqkv[
                        :, pl.ds(pl.multiple_of(g * 256 + part * WIDTH + b * LANES, LANES), LANES)
                    ] = piece
                else:
                    wout[:, pl.ds(pl.multiple_of(g * 256 + b * LANES, LANES), LANES)] = piece
    pos = recv_ref[:, FEAT_ROWS : FEAT_ROWS + POS_ROWS, :].reshape(SLOTS, LANES)
    pick = onehot(iota((16, LANES), 0) == iota((16, LANES), 1))
    digits = dot_t(pick, pos)
    place_row = (digits[0:1] * 32.0 + digits[1:2]).astype(jnp.int32) - 1
    arrive = onehot(iota((POINTS, SLOTS), 0) == place_row)
    for c in range(4):
        got = recv_ref[:, c * CAP : (c + 1) * CAP, :].reshape(SLOTS, LANES)
        hil[:, c * LANES : (c + 1) * LANES] = dot(arrive, got)
    rows = hil[...]
    centred = rows - jnp.mean(rows, axis=-1, keepdims=True)
    inv_scale = lax.rsqrt(jnp.mean(centred * centred, axis=-1, keepdims=True) + EPS)
    normed = (centred * inv_scale).astype(BF)
    nrm[...] = normed
    for part in range(6):
        cols = slice(part * 256, (part + 1) * 256)
        qkv[:, cols] = dot(normed, wqkv[:, cols]).astype(BF)
    cgrad[...] = dot_t(gout_ref[...], wout[...]).astype(BF)

    lane_head = iota((1, LANES), 1) // HEAD_CHANNELS

    def unit(u, carry):
        p = u // 4
        o = u % 4
        pts = pl.ds(pl.multiple_of(p * PATCH, PATCH), PATCH)
        lane = lambda part: pl.ds(pl.multiple_of(o * LANES + part * WIDTH, LANES), LANES)
        qs = qkv[pts, lane(0)] * BF(SCALE)
        k = qkv[pts, lane(1)]
        v = qkv[pts, lane(2)]
        dc = cgrad[pts, lane(0)]
        qs_t = qs.T
        ks_t = (k * BF(SCALE)).T
        v_t = v.T
        dc_t = dc.T
        for h in range(8):
            head = jnp.where(lane_head == h, 1.0, 0.0).astype(BF)
            chans = slice(h * HEAD_CHANNELS, (h + 1) * HEAD_CHANNELS)
            scores = dot_t(k * head, qs)
            exps = jnp.exp(scores - jnp.max(scores, axis=0, keepdims=True))
            probs = exps * (1.0 / jnp.sum(exps, axis=0, keepdims=True))
            probs_b = probs.astype(BF)
            prob_grad = dot_t(v * head, dc)
            total = jnp.sum(probs * prob_grad, axis=0, keepdims=True)
            score_grad = (probs * (prob_grad - total)).astype(BF)
            at = lambda part: pl.ds(
                pl.multiple_of(o * LANES + part * WIDTH + h * HEAD_CHANNELS, HEAD_CHANNELS),
                HEAD_CHANNELS,
            )
            ctx_t[at(0), pts] = dot(v_t[chans], probs_b).astype(BF)
            qg_t[at(0), pts] = dot(ks_t[chans], score_grad).astype(BF)
            qg_t[at(1), pts] = dot_t(qs_t[chans], score_grad).astype(BF)
            qg_t[at(2), pts] = dot_t(dc_t[chans], probs_b).astype(BF)
        return carry

    lax.fori_loop(0, 16, unit, 0)

    mixed_ref[...] = (hil[...] + dot(ctx_t[...].T, wout[...])).astype(BF)
    normed_t = nrm[...].T
    for g, ref in ((1 - group, send_ref), (group, keep_ref)):
        for part in range(3):
            chans = pl.ds(pl.multiple_of(g * 256 + part * WIDTH, 256), 256)
            term = dot_t(normed_t, qg_t[chans, :]).astype(BF)
            ref[2 * part] = term[:, :LANES]
            ref[2 * part + 1] = term[:, LANES:]
        cols = pl.ds(pl.multiple_of(g * 256, 256), 256)
        term = dot(ctx_t[...], gout_ref[:, cols]).astype(BF)
        ref[6] = term[:, :LANES]
        ref[7] = term[:, LANES:]
    rows = hil[...]
    centred = rows - jnp.mean(rows, axis=-1, keepdims=True)
    inv_scale = lax.rsqrt(jnp.mean(centred * centred, axis=-1, keepdims=True) + EPS)
    xhat = centred * inv_scale
    ngrad = dot(wqkv[...], qg_t[...]).T
    cent = ngrad - jnp.mean(ngrad, axis=-1, keepdims=True)
    cent = cent - xhat * jnp.mean(ngrad * xhat, axis=-1, keepdims=True)
    hgrad = (gout_ref[...].astype(F32) + inv_scale * cent).astype(BF)
    wide = pos.astype(F32)
    place_col = (wide[:, 0:1] * 32.0 + wide[:, 1:2]).astype(jnp.int32) - 1
    leave = onehot(iota((SLOTS, POINTS), 1) == place_col)
    for c in range(4):
        out = dot(leave, hgrad[:, c * LANES : (c + 1) * LANES]).astype(BF)
        back_ref[:, c * CAP : (c + 1) * CAP, :] = out.reshape(SHARDS, CAP, LANES)


def unpack_kernel(slot_ref, back_ref, out_ref):
    slot = slot_ref[0:1, :]
    row = iota((LANES, POINTS), 0)
    digits = jnp.where(row == 0, slot // 32, jnp.where(row == 1, slot % 32, 0))
    eye = onehot(iota((POINTS, POINTS), 0) == iota((POINTS, POINTS), 1))
    cols = dot_t(eye, digits.astype(F32).astype(BF))
    slot_col = (cols[:, 0:1] * 32.0 + cols[:, 1:2]).astype(jnp.int32)
    take = onehot(iota((POINTS, SLOTS), 1) == slot_col)
    for c in range(4):
        got = back_ref[:, c * CAP : (c + 1) * CAP, :].reshape(SLOTS, LANES)
        out_ref[:, c * LANES : (c + 1) * LANES] = dot(take, got).astype(BF)


VMEM = pl.BlockSpec(memory_space=pltpu.VMEM)
SMEM = pl.BlockSpec(memory_space=pltpu.SMEM)


def params(mib):
    return pltpu.CompilerParams(vmem_limit_bytes=mib * 1024 * 1024)


def exchange(array, axes):
    return lax.all_to_all(array, axes, split_axis=0, concat_axis=0, tiled=True)


def local(feats, hilbert_pos, w_qkv, w_out, grad_out):
    core = lax.axis_index("core").astype(jnp.int32)[None]
    send, slot = pl.pallas_call(
        pack_kernel,
        out_shape=(
            jax.ShapeDtypeStruct((SHARDS, SEND_ROWS, LANES), BF),
            jax.ShapeDtypeStruct((8, POINTS), jnp.int32),
        ),
        in_specs=[SMEM, VMEM, VMEM, VMEM, VMEM],
        out_specs=(VMEM, VMEM),
        compiler_params=params(32),
        name="pack",
    )(core, hilbert_pos, feats[0], w_qkv, w_out)
    recv = exchange(send, SEQ)
    swap = [(0, 1), (1, 0)]
    other = lax.ppermute(recv[:, FEAT_ROWS + POS_ROWS :, :], "core", swap)
    gout = grad_out[0]
    mixed, back, keep, give = pl.pallas_call(
        main_kernel,
        out_shape=(
            jax.ShapeDtypeStruct((POINTS, WIDTH), BF),
            jax.ShapeDtypeStruct((SHARDS, FEAT_ROWS, LANES), BF),
            jax.ShapeDtypeStruct((8, WIDTH, LANES), BF),
            jax.ShapeDtypeStruct((8, WIDTH, LANES), BF),
        ),
        in_specs=[SMEM, VMEM, VMEM, VMEM],
        out_specs=(VMEM, VMEM, VMEM, VMEM),
        scratch_shapes=[
            pltpu.VMEM((WIDTH, 3 * WIDTH), BF),
            pltpu.VMEM((WIDTH, WIDTH), BF),
            pltpu.VMEM((POINTS, WIDTH), F32),
            pltpu.VMEM((POINTS, WIDTH), BF),
            pltpu.VMEM((POINTS, 3 * WIDTH), BF),
            pltpu.VMEM((POINTS, WIDTH), BF),
            pltpu.VMEM((WIDTH, POINTS), BF),
            pltpu.VMEM((3 * WIDTH, POINTS), BF),
        ],
        compiler_params=params(50),
        name="attention",
    )(core, recv, other, gout)
    returned = exchange(back, SEQ)
    theirs = lax.ppermute(give, "core", swap)
    pair = (keep.astype(F32) + theirs.astype(F32)).astype(BF)
    by_y = exchange(pair, "y")
    share = jnp.sum(by_y.astype(F32), axis=0).astype(BF)
    by_seq = exchange(share.reshape(SHARDS, WIDTH // SHARDS, LANES), SEQ)
    factor = 1.0 / math.sqrt(16 * POINTS * SHARDS)
    total = jnp.sum(by_seq.astype(F32), axis=0) * factor
    whole = exchange(jnp.broadcast_to(total[None], (16,) + total.shape), BATCH)
    whole = whole.reshape(4, 2, 2, WIDTH // SHARDS, LANES)
    cols = whole.transpose(3, 0, 2, 1, 4).reshape(WIDTH // SHARDS, 4 * WIDTH)
    feat_grad = pl.pallas_call(
        unpack_kernel,
        out_shape=jax.ShapeDtypeStruct((POINTS, WIDTH), BF),
        in_specs=[VMEM, VMEM],
        out_specs=VMEM,
        compiler_params=params(32),
        name="unpack",
    )(slot, returned)
    return (mixed[None], feat_grad[None], cols[:, : 3 * WIDTH], cols[:, 3 * WIDTH :])


def solution(mesh):
    mesh = Mesh(mesh.devices.reshape(4, 8, 8, 2), ("x", "z", "y", "core"))
    rows = P(BATCH, SEQ, None)
    return jax.shard_map(
        local,
        mesh=mesh,
        in_specs=(rows, P(BATCH, SEQ), P(SEQ, None), P(SEQ, None), rows),
        out_specs=(rows, rows, P(SEQ, None), P(SEQ, None)),
        check_vma=False,
    )
```

```python
import math

import jax
import jax.numpy as jnp
from jax import lax
from jax.experimental import pallas as pl
from jax.experimental.pallas import tpu as pltpu
from jax.sharding import Mesh
from jax.sharding import PartitionSpec as P

HEADS = 32
HEAD_CHANNELS = 16
PATCH = 128
WIDTH = 512
POINTS = 512
SHARDS = 32
CAP = 32
SLOTS = SHARDS * CAP
LANES = 128
EPS = 1e-05
SCALE = HEAD_CHANNELS ** (-0.5)

BF = jnp.bfloat16
F32 = jnp.float32
SEQ = ("x", "z")
BATCH = ("y", "core")

FEAT_ROWS = 4 * CAP
SEND_ROWS = FEAT_ROWS + 16
W_COLS = 1024


def iota(shape, dim):
    return lax.broadcasted_iota(jnp.int32, shape, dim)


def onehot(condition):
    return jnp.where(condition, 1.0, 0.0).astype(BF)


def dot(left, right):
    return jnp.dot(left, right, preferred_element_type=F32)


def dot_t(left, right):
    return lax.dot_general(left, right, (((1,), (1,)), ((), ())), preferred_element_type=F32)


def pack_kernel(pos_ref, feats_ref, out_ref, slot_ref):
    target = pos_ref[...]
    owner = target // POINTS
    place = target % POINTS + 1
    mine = iota((SHARDS, POINTS), 0) == owner
    mine_b = onehot(mine)
    before = onehot(iota((POINTS, POINTS), 0) < iota((POINTS, POINTS), 1))
    ranks = dot(mine_b, before)
    rank = jnp.sum(jnp.where(mine, ranks, 0.0), axis=0, keepdims=True).astype(jnp.int32)
    slot = owner * CAP + rank
    slot_ref[...] = jnp.broadcast_to(slot, slot_ref.shape)
    place_of = onehot(iota((SLOTS, POINTS), 0) == slot)
    lane = iota((LANES, POINTS), 0)
    digits = jnp.where(lane == rank, place // 32, 0) + jnp.where(lane == rank + CAP, place % 32, 0)
    pos = dot_t(mine_b, digits.astype(F32).astype(BF)).astype(BF)
    out_ref[:, FEAT_ROWS:SEND_ROWS, :] = jnp.broadcast_to(pos[:, None, :], (SHARDS, 16, LANES))
    for c in range(4):
        rows = dot(place_of, feats_ref[:, c * LANES : (c + 1) * LANES]).astype(BF)
        out_ref[:, c * CAP : (c + 1) * CAP, :] = rows.reshape(SHARDS, CAP, LANES)


def positions(recv_ref):
    return recv_ref[:, FEAT_ROWS:SEND_ROWS, :][:, 0, :]


def arrivals(digits):
    lane, slot = iota((LANES, SLOTS), 0), iota((LANES, SLOTS), 1) % CAP
    spread = jnp.where(lane == slot, 32.0, jnp.where(lane == slot + CAP, 1.0, 0.0)).astype(BF)
    each = dot(digits, spread)
    source = iota((SHARDS, SLOTS), 0) == iota((SHARDS, SLOTS), 1) // CAP
    place = jnp.sum(jnp.where(source, each, 0.0), axis=0, keepdims=True).astype(jnp.int32) - 1
    return onehot(iota((POINTS, SLOTS), 0) == place)


def departures(digits):
    source = onehot(iota((SLOTS, SHARDS), 0) // CAP == iota((SLOTS, SHARDS), 1))
    each = dot(source, digits)
    slot, lane = iota((SLOTS, LANES), 0) % CAP, iota((SLOTS, LANES), 1)
    weight = jnp.where(lane == slot, 32.0, jnp.where(lane == slot + CAP, 1.0, 0.0))
    place = jnp.sum(each * weight, axis=1, keepdims=True).astype(jnp.int32) - 1
    return onehot(iota((SLOTS, POINTS), 1) == place)


def block_kernel(
    at_ref,
    recv_hbm,
    mine0_hbm,
    mine1_hbm,
    mine2_hbm,
    mine3_hbm,
    other_hbm,
    gout_hbm,
    mixed_hbm,
    keep_hbm,
    send_hbm,
    back_hbm,
    recv,
    w,
    gout,
    mixed,
    keep,
    send,
    back,
    hil,
    nrm,
    nrm_t,
    qkv,
    cgrad,
    ctx_t,
    qg_t,
    sems,
):
    group, x = at_ref[0], at_ref[1]
    copies = []

    def start(source, target):
        copy = pltpu.make_async_copy(source, target, sems.at[len(copies)])
        copy.start()
        copies.append(copy)
        return copy

    recv_copy = start(recv_hbm, recv)
    w_copies = []
    for k, mine in enumerate((mine0_hbm, mine1_hbm, mine2_hbm, mine3_hbm)):
        rows = pl.ds(pl.multiple_of(lax.rem(x + 4 - k, 4) * 128, 128), 128)
        w_copies.append(start(mine, w.at[group, rows, :]))
        w_copies.append(start(other_hbm.at[k], w.at[1 - group, rows, :]))
    gout_copy = start(gout_hbm, gout)

    recv_copy.wait()
    digits = positions(recv)
    arrive = arrivals(digits)
    for c in range(4):
        got = recv[:, c * CAP : (c + 1) * CAP, :].reshape(SLOTS, LANES)
        hil[:, c * LANES : (c + 1) * LANES] = dot(arrive, got)
    rows = hil[...]
    centred = rows - jnp.mean(rows, axis=-1, keepdims=True)
    inv_scale = lax.rsqrt(jnp.mean(centred * centred, axis=-1, keepdims=True) + EPS)
    normed = (centred * inv_scale).astype(BF)
    nrm[...] = normed
    for copy in w_copies:
        copy.wait()
    for g in range(2):
        for part in range(3):
            cols = slice(part * 256, (part + 1) * 256)
            at = slice(g * 768 + part * 256, g * 768 + (part + 1) * 256)
            qkv[:, at] = dot(normed, w[g, :, cols]).astype(BF)
    gout_copy.wait()
    cgrad[...] = (
        dot_t(gout[:, :256], w[0, :, 768:]) + dot_t(gout[:, 256:], w[1, :, 768:])
    ).astype(BF)

    by_lane = iota((1, LANES), 1) // HEAD_CHANNELS
    by_row = iota((LANES, 1), 0) // HEAD_CHANNELS
    lane_heads = [jnp.where(by_lane == h, 1.0, 0.0).astype(BF) for h in range(8)]
    row_heads = [jnp.where(by_row == h, 1.0, 0.0).astype(BF) for h in range(8)]

    def stack(array):
        return jnp.concatenate([array * head for head in lane_heads], axis=0)

    def spread(array):
        return jnp.concatenate([array * head for head in row_heads], axis=1)

    def unit(u, carry):
        p = u // 4
        o = u % 4
        pts = pl.ds(pl.multiple_of(p * PATCH, PATCH), PATCH)
        first = (o // 2) * 768 + (o % 2) * LANES
        block = lambda part: pl.ds(pl.multiple_of(first + part * 256, LANES), LANES)
        whole = pl.ds(pl.multiple_of(o * LANES, LANES), LANES)
        qs = qkv[pts, block(0)] * BF(SCALE)
        k = qkv[pts, block(1)]
        v = qkv[pts, block(2)]
        dc = cgrad[pts, whole]
        all_scores = dot_t(stack(k), qs)
        all_prob_grads = dot_t(stack(v), dc)
        probs_b, score_grads = [], []
        for h in range(8):
            scores = all_scores[h * PATCH : (h + 1) * PATCH]
            prob_grad = all_prob_grads[h * PATCH : (h + 1) * PATCH]
            exps = jnp.exp(scores - jnp.max(scores, axis=0, keepdims=True))
            probs = exps * (1.0 / jnp.sum(exps, axis=0, keepdims=True))
            total = jnp.sum(probs * prob_grad, axis=0, keepdims=True)
            probs_b.append(probs.astype(BF))
            score_grads.append((probs * (prob_grad - total)).astype(BF))
        rows_p, cols_p = jnp.concatenate(probs_b, axis=0), jnp.concatenate(probs_b, axis=1)
        rows_s, cols_s = jnp.concatenate(score_grads, axis=0), jnp.concatenate(score_grads, axis=1)
        ctx_t[whole, pts] = dot(spread(v.T), rows_p).astype(BF)
        qg_t[block(0), pts] = dot(spread((k * BF(SCALE)).T), rows_s).astype(BF)
        qg_t[block(1), pts] = dot(cols_s, stack(qs)).astype(BF).T
        qg_t[block(2), pts] = dot(cols_p, stack(dc)).astype(BF).T
        return carry

    lax.fori_loop(0, 16, unit, 0, unroll=2)

    nrm_t[...] = nrm[...].T
    for g, ref, target in ((1 - group, send, send_hbm), (group, keep, keep_hbm)):
        for k in range(4):
            rows = pl.ds(pl.multiple_of(lax.rem(x + k, 4) * 128, 128), 128)
            for part in range(3):
                chans = pl.ds(pl.multiple_of(g * 768 + part * 256, 256), 256)
                term = dot_t(nrm_t[rows, :], qg_t[chans, :]).astype(BF)
                ref[k, 2 * part] = term[:, :LANES]
                ref[k, 2 * part + 1] = term[:, LANES:]
            cols = pl.ds(pl.multiple_of(g * 256, 256), 256)
            term = dot(ctx_t[rows, :], gout[:, cols]).astype(BF)
            ref[k, 6] = term[:, :LANES]
            ref[k, 7] = term[:, LANES:]
        start(ref, target)
    context = ctx_t[...].T
    for g in range(2):
        cols = slice(g * 256, (g + 1) * 256)
        mixed[:, cols] = (hil[:, cols] + dot(context, w[g, :, 768:])).astype(BF)
    start(mixed, mixed_hbm)
    rows = hil[...]
    centred = rows - jnp.mean(rows, axis=-1, keepdims=True)
    inv_scale = lax.rsqrt(jnp.mean(centred * centred, axis=-1, keepdims=True) + EPS)
    xhat = centred * inv_scale
    ngrad = (dot(w[0, :, :768], qg_t[:768, :]) + dot(w[1, :, :768], qg_t[768:, :])).T
    cent = ngrad - jnp.mean(ngrad, axis=-1, keepdims=True)
    cent = cent - xhat * jnp.mean(ngrad * xhat, axis=-1, keepdims=True)
    hgrad = (gout[...].astype(F32) + inv_scale * cent).astype(BF)
    leave = departures(digits)
    for c in range(4):
        out = dot(leave, hgrad[:, c * LANES : (c + 1) * LANES]).astype(BF)
        back[:, c * CAP : (c + 1) * CAP, :] = out.reshape(SHARDS, CAP, LANES)
    start(back, back_hbm)
    for copy in copies[-4:]:
        copy.wait()


def pair_kernel(keep_ref, theirs_ref, *out_refs):
    for k in range(4):
        out_refs[k][...] = (keep_ref[k].astype(F32) + theirs_ref[k].astype(F32)).astype(BF)


def unpack_kernel(slot_ref, back_ref, out_ref):
    slot = slot_ref[0:1, :]
    row = iota((LANES, POINTS), 0)
    digits = jnp.where(row == 0, slot // 32, jnp.where(row == 1, slot % 32, 0))
    eye = onehot(iota((POINTS, POINTS), 0) == iota((POINTS, POINTS), 1))
    cols = dot_t(eye, digits.astype(F32).astype(BF))
    slot_col = (cols[:, 0:1] * 32.0 + cols[:, 1:2]).astype(jnp.int32)
    take = onehot(iota((POINTS, SLOTS), 1) == slot_col)
    for c in range(4):
        got = back_ref[:, c * CAP : (c + 1) * CAP, :].reshape(SLOTS, LANES)
        out_ref[:, c * LANES : (c + 1) * LANES] = dot(take, got).astype(BF)


VMEM = pl.BlockSpec(memory_space=pltpu.VMEM)
SMEM = pl.BlockSpec(memory_space=pltpu.SMEM)
ANY = pl.BlockSpec(memory_space=pl.ANY)


def params(mib):
    return pltpu.CompilerParams(vmem_limit_bytes=mib * 1024 * 1024)


def exchange(array, axes):
    return lax.all_to_all(array, axes, split_axis=0, concat_axis=0, tiled=True)


def cost(flops, size):
    return pl.CostEstimate(flops=flops, bytes_accessed=size, transcendentals=0)


def shift(array, axis, size, by):
    return lax.ppermute(array, axis, [(i, (i + by) % size) for i in range(size)])


def local(feats, hilbert_pos, w_qkv, w_out, grad_out):
    core, x = lax.axis_index("core"), lax.axis_index("x")
    at = jnp.stack([core, x]).astype(jnp.int32)
    pieces = [w_qkv[:, :WIDTH], w_qkv[:, WIDTH : 2 * WIDTH], w_qkv[:, 2 * WIDTH :], w_out]
    by_z = jnp.concatenate(
        [jnp.where(core == 0, piece[:, :256], piece[:, 256:]) for piece in pieces], axis=1
    )[None]
    by_z = exchange(jnp.broadcast_to(by_z, (8, 16, W_COLS)), "z").reshape(128, W_COLS)
    send, slot = pl.pallas_call(
        pack_kernel,
        out_shape=(
            jax.ShapeDtypeStruct((SHARDS, SEND_ROWS, LANES), BF),
            jax.ShapeDtypeStruct((8, POINTS), jnp.int32),
        ),
        in_specs=[VMEM, VMEM],
        out_specs=(VMEM, VMEM),
        compiler_params=params(32),
        cost_estimate=cost(10**9, 4 << 20),
        name="pack",
    )(hilbert_pos, feats[0])
    recv = exchange(send, SEQ)
    mine = [by_z] + [shift(by_z, "x", 4, k) for k in (1, 2, 3)]
    other = shift(jnp.stack(mine), "core", 2, 1)
    wgrad = jax.ShapeDtypeStruct((4, 8, LANES, LANES), BF)
    out_shape = (
        jax.ShapeDtypeStruct((POINTS, WIDTH), BF),
        wgrad,
        wgrad,
        jax.ShapeDtypeStruct((SHARDS, FEAT_ROWS, LANES), BF),
    )
    mixed, keep, give, back = pl.pallas_call(
        block_kernel,
        out_shape=out_shape,
        in_specs=[SMEM] + [ANY] * 7,
        out_specs=(ANY,) * 4,
        scratch_shapes=[
            pltpu.VMEM((SHARDS, SEND_ROWS, LANES), BF),
            pltpu.VMEM((2, WIDTH, W_COLS), BF),
            pltpu.VMEM((POINTS, WIDTH), BF),
            pltpu.VMEM((POINTS, WIDTH), BF),
            pltpu.VMEM(wgrad.shape, BF),
            pltpu.VMEM(wgrad.shape, BF),
            pltpu.VMEM((SHARDS, FEAT_ROWS, LANES), BF),
            pltpu.VMEM((POINTS, WIDTH), F32),
            pltpu.VMEM((POINTS, WIDTH), BF),
            pltpu.VMEM((WIDTH, POINTS), BF),
            pltpu.VMEM((POINTS, 3 * WIDTH), BF),
            pltpu.VMEM((POINTS, WIDTH), BF),
            pltpu.VMEM((WIDTH, POINTS), BF),
            pltpu.VMEM((3 * WIDTH, POINTS), BF),
            pltpu.SemaphoreType.DMA((14,)),
        ],
        compiler_params=params(50),
        cost_estimate=cost(10**10, 8 << 20),
        name="block",
    )(at, recv, *mine, other, grad_out[0])
    theirs = shift(give, "core", 2, 1)
    pair = pl.pallas_call(
        pair_kernel,
        out_shape=(jax.ShapeDtypeStruct((8, LANES, LANES), BF),) * 4,
        in_specs=[VMEM] * 2,
        out_specs=(VMEM,) * 4,
        compiler_params=params(32),
        cost_estimate=cost(10**6, 3 << 20),
        name="pair",
    )(keep, theirs)
    returned = exchange(back, SEQ)
    by_x = [pair[0]] + [shift(pair[k], "x", 4, k) for k in (1, 2, 3)]
    *by_x, returned = lax.optimization_barrier((*by_x, returned))
    share = sum(term.astype(F32) for term in by_x).astype(BF)
    by_z = exchange(share.reshape(8, 8, 16, LANES).transpose(1, 2, 0, 3), "z")
    part = jnp.sum(by_z.astype(F32), axis=0).astype(BF)
    by_y = exchange(jnp.broadcast_to(part[None], (8,) + part.shape), "y")
    factor = 1.0 / math.sqrt(16 * POINTS * SHARDS)
    total = jnp.sum(by_y.astype(F32), axis=0).reshape(16, W_COLS) * factor
    theirs = shift(total, "core", 2, 1)
    halves = [jnp.where(core == 0, total, theirs), jnp.where(core == 0, theirs, total)]
    qkv_wgrad = jnp.concatenate(
        [half[:, part * 256 : (part + 1) * 256] for part in range(3) for half in halves], axis=1
    )
    out_wgrad = jnp.concatenate([half[:, 768:] for half in halves], axis=1)
    feat_grad = pl.pallas_call(
        unpack_kernel,
        out_shape=jax.ShapeDtypeStruct((POINTS, WIDTH), BF),
        in_specs=[VMEM, VMEM],
        out_specs=VMEM,
        compiler_params=params(32),
        cost_estimate=cost(10**9, 4 << 20),
        name="unpack",
    )(slot, returned)
    return (mixed[None], feat_grad[None], qkv_wgrad, out_wgrad)


def solution(mesh):
    mesh = Mesh(mesh.devices.reshape(4, 8, 8, 2), ("x", "z", "y", "core"))
    rows = P(BATCH, SEQ, None)
    return jax.shard_map(
        local,
        mesh=mesh,
        in_specs=(rows, P(BATCH, SEQ), P(SEQ, None), P(SEQ, None), rows),
        out_specs=(rows, rows, P(SEQ, None), P(SEQ, None)),
        check_vma=False,
    )
```

```python
import math

import jax
import jax.numpy as jnp
from jax import lax
from jax.experimental import pallas as pl
from jax.experimental.pallas import tpu as pltpu
from jax.sharding import Mesh
from jax.sharding import PartitionSpec as P

HEADS = 32
HEAD_CHANNELS = 16
PATCH = 128
WIDTH = 512
POINTS = 512
SHARDS = 32
CAP = 32
SLOTS = SHARDS * CAP
LANES = 128
EPS = 1e-05
SCALE = HEAD_CHANNELS ** (-0.5)

BF = jnp.bfloat16
F32 = jnp.float32
SEQ = ("x", "z")
BATCH = ("y", "core")

FEAT_ROWS = 4 * CAP
SEND_ROWS = FEAT_ROWS + 16
W_COLS = 1024


def iota(shape, dim):
    return lax.broadcasted_iota(jnp.int32, shape, dim)


def onehot(condition):
    return jnp.where(condition, 1.0, 0.0).astype(BF)


def dot(left, right):
    return jnp.dot(left, right, preferred_element_type=F32)


def dot_t(left, right):
    return lax.dot_general(left, right, (((1,), (1,)), ((), ())), preferred_element_type=F32)


def pack_kernel(pos_ref, feats_ref, out_ref, slot_ref):
    target = pos_ref[...]
    owner = target // POINTS
    place = target % POINTS + 1
    mine = iota((SHARDS, POINTS), 0) == owner
    mine_b = onehot(mine)
    before = onehot(iota((POINTS, POINTS), 0) < iota((POINTS, POINTS), 1))
    ranks = dot(mine_b, before)
    rank = jnp.sum(jnp.where(mine, ranks, 0.0), axis=0, keepdims=True).astype(jnp.int32)
    slot = owner * CAP + rank
    slot_ref[...] = jnp.broadcast_to(slot, slot_ref.shape)
    place_of = onehot(iota((SLOTS, POINTS), 0) == slot)
    lane = iota((LANES, POINTS), 0)
    digits = jnp.where(lane == rank, place // 32, 0) + jnp.where(lane == rank + CAP, place % 32, 0)
    pos = dot_t(mine_b, digits.astype(F32).astype(BF)).astype(BF)
    out_ref[:, FEAT_ROWS:SEND_ROWS, :] = jnp.broadcast_to(pos[:, None, :], (SHARDS, 16, LANES))
    for c in range(0, 4, 2):
        rows = dot(place_of, feats_ref[:, c * LANES : (c + 2) * LANES]).astype(BF)
        for b in range(2):
            block = rows[:, b * LANES : (b + 1) * LANES]
            out_ref[:, (c + b) * CAP : (c + b + 1) * CAP, :] = block.reshape(SHARDS, CAP, LANES)


def positions(recv_ref):
    return recv_ref[:, FEAT_ROWS:SEND_ROWS, :][:, 0, :]


def slot_rows(ref, c):
    blocks = [
        ref[:, b * CAP : (b + 1) * CAP, :].reshape(SLOTS, LANES) for b in (c, c + 1)
    ]
    return jnp.concatenate(blocks, axis=1)


def arrivals(digits):
    lane, slot = iota((LANES, SLOTS), 0), iota((LANES, SLOTS), 1) % CAP
    spread = jnp.where(lane == slot, 32.0, jnp.where(lane == slot + CAP, 1.0, 0.0)).astype(BF)
    each = dot(digits, spread)
    source = iota((SHARDS, SLOTS), 0) == iota((SHARDS, SLOTS), 1) // CAP
    place = jnp.sum(jnp.where(source, each, 0.0), axis=0, keepdims=True).astype(jnp.int32) - 1
    return onehot(iota((POINTS, SLOTS), 0) == place)


def departures(digits):
    source = onehot(iota((SLOTS, SHARDS), 0) // CAP == iota((SLOTS, SHARDS), 1))
    each = dot(source, digits)
    slot, lane = iota((SLOTS, LANES), 0) % CAP, iota((SLOTS, LANES), 1)
    weight = jnp.where(lane == slot, 32.0, jnp.where(lane == slot + CAP, 1.0, 0.0))
    place = jnp.sum(each * weight, axis=1, keepdims=True).astype(jnp.int32) - 1
    return onehot(iota((SLOTS, POINTS), 1) == place)


def arrive_kernel(recv, hil, nrm, digits_ref):
    digits = positions(recv)
    digits_ref[...] = digits
    arrive = arrivals(digits)
    rows = []
    for c in range(0, 4, 2):
        rows.append(dot(arrive, slot_rows(recv, c)))
        hil[:, c * LANES : (c + 2) * LANES] = rows[-1].astype(BF)
    rows = jnp.concatenate(rows, axis=1)
    centred = rows - jnp.mean(rows, axis=-1, keepdims=True)
    inv_scale = lax.rsqrt(jnp.mean(centred * centred, axis=-1, keepdims=True) + EPS)
    nrm[...] = (centred * inv_scale).astype(BF)


def block_kernel(
    at_ref,
    hil,
    nrm,
    digits_ref,
    mine0_ref,
    mine1_ref,
    mine2_ref,
    mine3_ref,
    other_ref,
    gout_hbm,
    mixed_hbm,
    keep_hbm,
    send_hbm,
    back_hbm,
    w,
    gout,
    mixed,
    keep,
    send,
    back,
    nrm_t,
    qkv,
    cgrad,
    ctx_t,
    qg_t,
    sd,
    sems,
):
    group, x = at_ref[0], at_ref[1]
    copies = []

    def start(source, target):
        copy = pltpu.make_async_copy(source, target, sems.at[len(copies)])
        copy.start()
        copies.append(copy)
        return copy

    w_copies = []
    for k, mine in enumerate((mine0_ref, mine1_ref, mine2_ref, mine3_ref)):
        rows = pl.ds(pl.multiple_of(lax.rem(x + 4 - k, 4) * 128, 128), 128)
        w_copies.append(start(mine, w.at[group, rows, :]))
        w_copies.append(start(other_ref.at[k], w.at[1 - group, rows, :]))
    gout_copy = start(gout_hbm, gout)
    nrm_t[...] = nrm[...].T
    normed = nrm[...]
    for copy in w_copies:
        copy.wait()
    for g in range(2):
        for part in range(3):
            cols = slice(part * 256, (part + 1) * 256)
            at = slice(g * 768 + part * 256, g * 768 + (part + 1) * 256)
            qkv[:, at] = dot(normed, w[g, :, cols]).astype(BF)
    gout_copy.wait()
    cgrad[...] = (
        dot_t(gout[:, :256], w[0, :, 768:]) + dot_t(gout[:, 256:], w[1, :, 768:])
    ).astype(BF)

    by_lane = iota((1, LANES), 1) // HEAD_CHANNELS
    by_row = iota((LANES, 1), 0) // HEAD_CHANNELS
    lane_heads = [jnp.where(by_lane == h, 1.0, 0.0).astype(BF) for h in range(8)]
    row_heads = [jnp.where(by_row == h, 1.0, 0.0).astype(BF) for h in range(8)]

    def stack(array):
        return jnp.concatenate([array * head for head in lane_heads], axis=0)

    def spread(array):
        return jnp.concatenate([array * head for head in row_heads], axis=1)

    def places(u):
        p = u // 4
        o = u % 4
        pts = pl.ds(pl.multiple_of(p * PATCH, PATCH), PATCH)
        first = (o // 2) * 768 + (o % 2) * LANES
        block = lambda part: pl.ds(pl.multiple_of(first + part * 256, LANES), LANES)
        whole = pl.ds(pl.multiple_of(o * LANES, LANES), LANES)
        return pts, block, whole

    def scores_of(u, slot):
        pts, block, whole = places(u)
        sd[slot, 0] = dot_t(stack(qkv[pts, block(1)]), qkv[pts, block(0)] * BF(SCALE))
        sd[slot, 1] = dot_t(stack(qkv[pts, block(2)]), cgrad[pts, whole])

    def unit(u, slot):
        pts, block, whole = places(u)
        qs = qkv[pts, block(0)] * BF(SCALE)
        k = qkv[pts, block(1)]
        v = qkv[pts, block(2)]
        dc = cgrad[pts, whole]
        probs_b, score_grads = [], []
        for h in range(8):
            scores = sd[slot, 0, h * PATCH : (h + 1) * PATCH, :]
            prob_grad = sd[slot, 1, h * PATCH : (h + 1) * PATCH, :]
            exps = jnp.exp(scores - jnp.max(scores, axis=0, keepdims=True))
            probs = exps * (1.0 / jnp.sum(exps, axis=0, keepdims=True))
            total = jnp.sum(probs * prob_grad, axis=0, keepdims=True)
            probs_b.append(probs.astype(BF))
            score_grads.append((probs * (prob_grad - total)).astype(BF))
        rows_p, cols_p = jnp.concatenate(probs_b, axis=0), jnp.concatenate(probs_b, axis=1)
        rows_s, cols_s = jnp.concatenate(score_grads, axis=0), jnp.concatenate(score_grads, axis=1)
        both = dot(
            jnp.concatenate([spread(v.T), spread((k * BF(SCALE)).T)], axis=0),
            jnp.concatenate([rows_p, rows_s], axis=1),
        ).astype(BF)
        ctx_t[whole, pts] = both[:LANES, :PATCH]
        qg_t[block(0), pts] = both[LANES:, PATCH:]
        qg_t[block(1), pts] = dot(cols_s, stack(qs)).astype(BF).T
        qg_t[block(2), pts] = dot(cols_p, stack(dc)).astype(BF).T

    def two_units(t, carry):
        scores_of(2 * t + 1, 1)
        unit(2 * t, 0)
        scores_of(jnp.minimum(2 * t + 2, 15), 0)
        unit(2 * t + 1, 1)
        return carry

    scores_of(0, 0)
    lax.fori_loop(0, 8, two_units, 0, unroll=2)

    def keep_term(ref, part, term):
        for b in range(4):
            k = lax.rem(b + 4 - x, 4)
            rows = slice(b * LANES, (b + 1) * LANES)
            ref[k, 2 * part] = term[rows, :LANES]
            ref[k, 2 * part + 1] = term[rows, LANES:]

    for g, ref, target in ((1 - group, send, send_hbm), (group, keep, keep_hbm)):
        for part in range(3):
            chans = pl.ds(pl.multiple_of(g * 768 + part * 256, 256), 256)
            keep_term(ref, part, dot_t(nrm_t[...], qg_t[chans, :]).astype(BF))
        cols = pl.ds(pl.multiple_of(g * 256, 256), 256)
        keep_term(ref, 3, dot(ctx_t[...], gout[:, cols]).astype(BF))
        start(ref, target)
    context = ctx_t[...].T
    for g in range(2):
        cols = slice(g * 256, (g + 1) * 256)
        mixed[:, cols] = (hil[:, cols].astype(F32) + dot(context, w[g, :, 768:])).astype(BF)
    start(mixed, mixed_hbm)
    rows = hil[...].astype(F32)
    centred = rows - jnp.mean(rows, axis=-1, keepdims=True)
    inv_scale = lax.rsqrt(jnp.mean(centred * centred, axis=-1, keepdims=True) + EPS)
    xhat = centred * inv_scale
    ngrad = (dot(w[0, :, :768], qg_t[:768, :]) + dot(w[1, :, :768], qg_t[768:, :])).T
    cent = ngrad - jnp.mean(ngrad, axis=-1, keepdims=True)
    cent = cent - xhat * jnp.mean(ngrad * xhat, axis=-1, keepdims=True)
    hgrad = (gout[...].astype(F32) + inv_scale * cent).astype(BF)
    leave = departures(digits_ref[...])
    for c in range(0, 4, 2):
        out = dot(leave, hgrad[:, c * LANES : (c + 2) * LANES]).astype(BF)
        for b in range(2):
            block = out[:, b * LANES : (b + 1) * LANES]
            back[:, (c + b) * CAP : (c + b + 1) * CAP, :] = block.reshape(SHARDS, CAP, LANES)
    start(back, back_hbm)
    for copy in copies[-4:]:
        copy.wait()


def pair_kernel(keep_ref, theirs_ref, *out_refs):
    for k in range(4):
        out_refs[k][...] = (keep_ref[k].astype(F32) + theirs_ref[k].astype(F32)).astype(BF)


def columns_kernel(blocks_ref, qkv_ref, out_ref):
    for y in range(8):
        for core in range(2):
            first = y // 2 * WIDTH + core * 256 + y % 2 * LANES
            block = blocks_ref[2 * y + core]
            if first < 3 * WIDTH:
                qkv_ref[:, first : first + LANES] = block
            else:
                out_ref[:, first - 3 * WIDTH : first - 3 * WIDTH + LANES] = block


def unpack_kernel(slot_ref, back_ref, out_ref):
    slot = slot_ref[0:1, :]
    row = iota((LANES, POINTS), 0)
    digits = jnp.where(row == 0, slot // 32, jnp.where(row == 1, slot % 32, 0))
    eye = onehot(iota((POINTS, POINTS), 0) == iota((POINTS, POINTS), 1))
    cols = dot_t(eye, digits.astype(F32).astype(BF))
    slot_col = (cols[:, 0:1] * 32.0 + cols[:, 1:2]).astype(jnp.int32)
    take = onehot(iota((POINTS, SLOTS), 1) == slot_col)
    for c in range(0, 4, 2):
        out_ref[:, c * LANES : (c + 2) * LANES] = dot(take, slot_rows(back_ref, c)).astype(BF)


VMEM = pl.BlockSpec(memory_space=pltpu.VMEM)
SMEM = pl.BlockSpec(memory_space=pltpu.SMEM)
ANY = pl.BlockSpec(memory_space=pl.ANY)
HBM = pl.BlockSpec(memory_space=pltpu.HBM)


def params(mib):
    return pltpu.CompilerParams(vmem_limit_bytes=mib * 1024 * 1024)


def exchange(array, axes):
    return lax.all_to_all(array, axes, split_axis=0, concat_axis=0, tiled=True)


def cost(flops, size):
    return pl.CostEstimate(flops=flops, bytes_accessed=size, transcendentals=0)


def shift(array, axis, size, by):
    return lax.ppermute(array, axis, [(i, (i + by) % size) for i in range(size)])


def local(feats, hilbert_pos, w_qkv, w_out, grad_out):
    core, x = lax.axis_index("core"), lax.axis_index("x")
    at = jnp.stack([core, x]).astype(jnp.int32)
    pieces = [w_qkv[:, :WIDTH], w_qkv[:, WIDTH : 2 * WIDTH], w_qkv[:, 2 * WIDTH :], w_out]
    by_z = jnp.concatenate(
        [jnp.where(core == 0, piece[:, :256], piece[:, 256:]) for piece in pieces], axis=1
    )[None]
    by_z = exchange(jnp.broadcast_to(by_z, (8, 16, W_COLS)), "z").reshape(128, W_COLS)
    send, slot = pl.pallas_call(
        pack_kernel,
        out_shape=(
            jax.ShapeDtypeStruct((SHARDS, SEND_ROWS, LANES), BF),
            jax.ShapeDtypeStruct((8, POINTS), jnp.int32),
        ),
        in_specs=[VMEM, VMEM],
        out_specs=(VMEM, VMEM),
        compiler_params=params(32),
        cost_estimate=cost(10**9, 4 << 20),
        name="pack",
    )(hilbert_pos, feats[0])
    recv = exchange(send, SEQ)
    mine = [by_z] + [shift(by_z, "x", 4, k) for k in (1, 2, 3)]
    other = shift(jnp.stack(mine), "core", 2, 1)
    wgrad = jax.ShapeDtypeStruct((4, 8, LANES, LANES), BF)
    out_shape = (
        jax.ShapeDtypeStruct((POINTS, WIDTH), BF),
        wgrad,
        wgrad,
        jax.ShapeDtypeStruct((SHARDS, FEAT_ROWS, LANES), BF),
    )
    hilbert, normed, digits = pl.pallas_call(
        arrive_kernel,
        out_shape=(
            jax.ShapeDtypeStruct((POINTS, WIDTH), BF),
            jax.ShapeDtypeStruct((POINTS, WIDTH), BF),
            jax.ShapeDtypeStruct((SHARDS, LANES), BF),
        ),
        in_specs=[VMEM],
        out_specs=(VMEM,) * 3,
        compiler_params=params(32),
        cost_estimate=cost(2 * 10**9, 4 << 20),
        name="arrive",
    )(recv)
    mixed, keep, give, back = pl.pallas_call(
        block_kernel,
        out_shape=out_shape,
        in_specs=[SMEM] + [VMEM] * 8 + [HBM],
        out_specs=(ANY,) * 4,
        scratch_shapes=[
            pltpu.VMEM((2, WIDTH, W_COLS), BF),
            pltpu.VMEM((POINTS, WIDTH), BF),
            pltpu.VMEM((POINTS, WIDTH), BF),
            pltpu.VMEM(wgrad.shape, BF),
            pltpu.VMEM(wgrad.shape, BF),
            pltpu.VMEM((SHARDS, FEAT_ROWS, LANES), BF),
            pltpu.VMEM((WIDTH, POINTS), BF),
            pltpu.VMEM((POINTS, 3 * WIDTH), BF),
            pltpu.VMEM((POINTS, WIDTH), BF),
            pltpu.VMEM((WIDTH, POINTS), BF),
            pltpu.VMEM((3 * WIDTH, POINTS), BF),
            pltpu.VMEM((2, 2, 8 * PATCH, PATCH), F32),
            pltpu.SemaphoreType.DMA((13,)),
        ],
        compiler_params=params(50),
        cost_estimate=cost(10**10, 8 << 20),
        name="block",
    )(at, hilbert, normed, digits, *mine, other, grad_out[0])
    theirs = shift(give, "core", 2, 1)
    pair = pl.pallas_call(
        pair_kernel,
        out_shape=(jax.ShapeDtypeStruct((8, LANES, LANES), BF),) * 4,
        in_specs=[VMEM, VMEM],
        out_specs=(VMEM,) * 4,
        compiler_params=params(32),
        cost_estimate=cost(10**6, 3 << 20),
        name="pair",
    )(keep, theirs)
    returned = exchange(back, SEQ)
    by_x = [pair[0]] + [shift(pair[k], "x", 4, k) for k in (1, 2, 3)]
    *by_x, returned = lax.optimization_barrier((*by_x, returned))
    share = sum(term.astype(F32) for term in by_x).astype(BF)
    by_seq = exchange(share.reshape(64, WIDTH // SHARDS, LANES), ("y", "z"))
    factor = 1.0 / math.sqrt(16 * POINTS * SHARDS)
    total = jnp.sum(by_seq.astype(F32), axis=0) * factor
    whole = exchange(jnp.broadcast_to(total[None], (16,) + total.shape), BATCH)
    qkv_wgrad, out_wgrad = pl.pallas_call(
        columns_kernel,
        out_shape=(
            jax.ShapeDtypeStruct((WIDTH // SHARDS, 3 * WIDTH), F32),
            jax.ShapeDtypeStruct((WIDTH // SHARDS, WIDTH), F32),
        ),
        in_specs=[VMEM],
        out_specs=(VMEM, VMEM),
        compiler_params=params(32),
        cost_estimate=cost(10**6, 1 << 18),
        name="columns",
    )(whole)
    feat_grad = pl.pallas_call(
        unpack_kernel,
        out_shape=jax.ShapeDtypeStruct((POINTS, WIDTH), BF),
        in_specs=[VMEM, VMEM],
        out_specs=VMEM,
        compiler_params=params(32),
        cost_estimate=cost(10**9, 4 << 20),
        name="unpack",
    )(slot, returned)
    return (mixed[None], feat_grad[None], qkv_wgrad, out_wgrad)


def solution(mesh):
    mesh = Mesh(mesh.devices.reshape(4, 8, 8, 2), ("x", "z", "y", "core"))
    rows = P(BATCH, SEQ, None)
    return jax.shard_map(
        local,
        mesh=mesh,
        in_specs=(rows, P(BATCH, SEQ), P(SEQ, None), P(SEQ, None), rows),
        out_specs=(rows, rows, P(SEQ, None), P(SEQ, None)),
        check_vma=False,
    )
```

```python
import functools
import math

import jax
import jax.numpy as jnp
from jax import lax
from jax.experimental import pallas as pl
from jax.experimental.pallas import tpu as pltpu
from jax.sharding import Mesh
from jax.sharding import PartitionSpec as P

HEADS = 32
HEAD_CHANNELS = 16
PATCH = 128
WIDTH = 512
POINTS = 512
SHARDS = 32
CAP = 32
SLOTS = SHARDS * CAP
LANES = 128
EPS = 1e-05
SCALE = HEAD_CHANNELS ** (-0.5)

BF = jnp.bfloat16
F32 = jnp.float32
SEQ = ("x", "z")
BATCH = ("y", "core")

FEAT_ROWS = 4 * CAP
SEND_ROWS = FEAT_ROWS + 16
W_COLS = 1024
X_SHIFTS = (0, 1, 3, 2)


def iota(shape, dim):
    return lax.broadcasted_iota(jnp.int32, shape, dim)


def onehot(condition):
    return jnp.where(condition, 1.0, 0.0).astype(BF)


def dot(left, right):
    return jnp.dot(left, right, preferred_element_type=F32)


def dot_t(left, right):
    return lax.dot_general(left, right, (((1,), (1,)), ((), ())), preferred_element_type=F32)


def pack_kernel(pos_ref, feats_ref, out_ref, slot_ref):
    target = pos_ref[...]
    owner = target // POINTS
    place = target % POINTS + 1
    mine = iota((SHARDS, POINTS), 0) == owner
    mine_b = onehot(mine)
    before = onehot(iota((POINTS, POINTS), 0) < iota((POINTS, POINTS), 1))
    ranks = dot(mine_b, before)
    rank = jnp.sum(jnp.where(mine, ranks, 0.0), axis=0, keepdims=True).astype(jnp.int32)
    slot = owner * CAP + rank
    slot_ref[...] = jnp.broadcast_to(slot, slot_ref.shape)
    place_of = onehot(iota((SLOTS, POINTS), 0) == slot)
    lane = iota((LANES, POINTS), 0)
    digits = jnp.where(lane == rank, place // 32, 0) + jnp.where(lane == rank + CAP, place % 32, 0)
    pos = dot_t(mine_b, digits.astype(F32).astype(BF)).astype(BF)
    out_ref[:, FEAT_ROWS:SEND_ROWS, :] = jnp.broadcast_to(pos[:, None, :], (SHARDS, 16, LANES))
    for c in range(0, 4, 2):
        rows = dot(place_of, feats_ref[:, c * LANES : (c + 2) * LANES]).astype(BF)
        for b in range(2):
            block = rows[:, b * LANES : (b + 1) * LANES]
            out_ref[:, (c + b) * CAP : (c + b + 1) * CAP, :] = block.reshape(SHARDS, CAP, LANES)


def positions(recv_ref):
    return recv_ref[:, FEAT_ROWS:SEND_ROWS, :][:, 0, :]


def slot_rows(ref, c):
    blocks = [
        ref[:, b * CAP : (b + 1) * CAP, :].reshape(SLOTS, LANES) for b in (c, c + 1)
    ]
    return jnp.concatenate(blocks, axis=1)


def arrivals(digits):
    lane, slot = iota((LANES, SLOTS), 0), iota((LANES, SLOTS), 1) % CAP
    spread = jnp.where(lane == slot, 32.0, jnp.where(lane == slot + CAP, 1.0, 0.0)).astype(BF)
    each = dot(digits, spread)
    source = iota((SHARDS, SLOTS), 0) == iota((SHARDS, SLOTS), 1) // CAP
    place = jnp.sum(jnp.where(source, each, 0.0), axis=0, keepdims=True).astype(jnp.int32) - 1
    return onehot(iota((POINTS, SLOTS), 0) == place)


def departures(digits):
    source = onehot(iota((SLOTS, SHARDS), 0) // CAP == iota((SLOTS, SHARDS), 1))
    each = dot(source, digits)
    slot, lane = iota((SLOTS, LANES), 0) % CAP, iota((SLOTS, LANES), 1)
    weight = jnp.where(lane == slot, 32.0, jnp.where(lane == slot + CAP, 1.0, 0.0))
    place = jnp.sum(each * weight, axis=1, keepdims=True).astype(jnp.int32) - 1
    return onehot(iota((SLOTS, POINTS), 1) == place)


def arrive_kernel(recv, hil, nrm, digits_ref):
    digits = positions(recv)
    digits_ref[...] = digits
    arrive = arrivals(digits)
    rows = []
    for c in range(0, 4, 2):
        rows.append(dot(arrive, slot_rows(recv, c)))
        hil[:, c * LANES : (c + 2) * LANES] = rows[-1].astype(BF)
    rows = jnp.concatenate(rows, axis=1)
    centred = rows - jnp.mean(rows, axis=-1, keepdims=True)
    inv_scale = lax.rsqrt(jnp.mean(centred * centred, axis=-1, keepdims=True) + EPS)
    nrm[...] = (centred * inv_scale).astype(BF)


def block_kernel(
    at_ref,
    hil,
    nrm,
    digits_ref,
    mine0_ref,
    mine1_ref,
    mine2_ref,
    mine3_ref,
    other_ref,
    gout_hbm,
    mixed_hbm,
    keep,
    send,
    back_hbm,
    w,
    gout,
    mixed,
    back,
    nrm_t,
    qkv,
    cgrad,
    ctx_t,
    qg_t,
    sd,
    sems,
):
    group, x = at_ref[0], at_ref[1]
    copies = []

    def start(source, target):
        copy = pltpu.make_async_copy(source, target, sems.at[len(copies)])
        copy.start()
        copies.append(copy)
        return copy

    w_copies = []
    for k, mine in enumerate((mine0_ref, mine1_ref, mine2_ref, mine3_ref)):
        rows = pl.ds(pl.multiple_of(lax.rem(x + 4 - X_SHIFTS[k], 4) * 128, 128), 128)
        w_copies.append(start(mine, w.at[group, rows, :]))
        w_copies.append(start(other_ref.at[k], w.at[1 - group, rows, :]))
    gout_copy = start(gout_hbm, gout)
    nrm_t[...] = nrm[...].T
    normed = nrm[...]
    for copy in w_copies:
        copy.wait()
    for g in range(2):
        for part in range(3):
            cols = slice(part * 256, (part + 1) * 256)
            at = slice(g * 768 + part * 256, g * 768 + (part + 1) * 256)
            qkv[:, at] = dot(normed, w[g, :, cols]).astype(BF)
    gout_copy.wait()
    cgrad[...] = (
        dot_t(gout[:, :256], w[0, :, 768:]) + dot_t(gout[:, 256:], w[1, :, 768:])
    ).astype(BF)

    by_lane = iota((1, LANES), 1) // HEAD_CHANNELS
    by_row = iota((LANES, 1), 0) // HEAD_CHANNELS
    lane_heads = [jnp.where(by_lane == h, 1.0, 0.0).astype(BF) for h in range(8)]
    row_heads = [jnp.where(by_row == h, 1.0, 0.0).astype(BF) for h in range(8)]

    def stack(array):
        return jnp.concatenate([array * head for head in lane_heads], axis=0)

    def spread(array):
        return jnp.concatenate([array * head for head in row_heads], axis=1)

    def places(u):
        p = u // 4
        o = u % 4
        pts = pl.ds(pl.multiple_of(p * PATCH, PATCH), PATCH)
        first = (o // 2) * 768 + (o % 2) * LANES
        block = lambda part: pl.ds(pl.multiple_of(first + part * 256, LANES), LANES)
        whole = pl.ds(pl.multiple_of(o * LANES, LANES), LANES)
        return pts, block, whole

    def scores_of(u, slot):
        pts, block, whole = places(u)
        sd[slot, 0] = dot_t(stack(qkv[pts, block(1)]), qkv[pts, block(0)] * BF(SCALE))
        sd[slot, 1] = dot_t(stack(qkv[pts, block(2)]), cgrad[pts, whole])

    def unit(u, slot):
        pts, block, whole = places(u)
        qs = qkv[pts, block(0)] * BF(SCALE)
        k = qkv[pts, block(1)]
        v = qkv[pts, block(2)]
        dc = cgrad[pts, whole]
        probs_b, score_grads = [], []
        for h in range(8):
            scores = sd[slot, 0, h * PATCH : (h + 1) * PATCH, :]
            prob_grad = sd[slot, 1, h * PATCH : (h + 1) * PATCH, :]
            exps = jnp.exp(scores - jnp.max(scores, axis=0, keepdims=True))
            probs = exps * (1.0 / jnp.sum(exps, axis=0, keepdims=True))
            total = jnp.sum(probs * prob_grad, axis=0, keepdims=True)
            probs_b.append(probs.astype(BF))
            score_grads.append((probs * (prob_grad - total)).astype(BF))
        rows_p, cols_p = jnp.concatenate(probs_b, axis=0), jnp.concatenate(probs_b, axis=1)
        rows_s, cols_s = jnp.concatenate(score_grads, axis=0), jnp.concatenate(score_grads, axis=1)
        both = dot(
            jnp.concatenate([spread(v.T), spread((k * BF(SCALE)).T)], axis=0),
            jnp.concatenate([rows_p, rows_s], axis=1),
        ).astype(BF)
        ctx_t[whole, pts] = both[:LANES, :PATCH]
        qg_t[block(0), pts] = both[LANES:, PATCH:]
        both = dot(
            jnp.concatenate([cols_s, cols_p], axis=0),
            jnp.concatenate([stack(qs), stack(dc)], axis=1),
        ).astype(BF)
        qg_t[block(1), pts] = both[:PATCH, :LANES].T
        qg_t[block(2), pts] = both[PATCH:, LANES:].T

    def two_units(t, carry):
        scores_of(2 * t + 1, 1)
        unit(2 * t, 0)
        scores_of(jnp.minimum(2 * t + 2, 15), 0)
        unit(2 * t + 1, 1)
        return carry

    scores_of(0, 0)
    lax.fori_loop(0, 8, two_units, 0, unroll=4)

    rows = hil[...].astype(F32)
    centred = rows - jnp.mean(rows, axis=-1, keepdims=True)
    inv_scale = lax.rsqrt(jnp.mean(centred * centred, axis=-1, keepdims=True) + EPS)
    xhat = centred * inv_scale
    ngrad = (dot(w[0, :, :768], qg_t[:768, :]) + dot(w[1, :, :768], qg_t[768:, :])).T
    cent = ngrad - jnp.mean(ngrad, axis=-1, keepdims=True)
    cent = cent - xhat * jnp.mean(ngrad * xhat, axis=-1, keepdims=True)
    hgrad = (gout[...].astype(F32) + inv_scale * cent).astype(BF)
    leave = departures(digits_ref[...])
    for c in range(0, 4, 2):
        out = dot(leave, hgrad[:, c * LANES : (c + 2) * LANES]).astype(BF)
        for b in range(2):
            block = out[:, b * LANES : (b + 1) * LANES]
            back[:, (c + b) * CAP : (c + b + 1) * CAP, :] = block.reshape(SHARDS, CAP, LANES)
    start(back, back_hbm)
    context = ctx_t[...].T
    for g in range(2):
        cols = slice(g * 256, (g + 1) * 256)
        mixed[:, cols] = (hil[:, cols].astype(F32) + dot(context, w[g, :, 768:])).astype(BF)
    start(mixed, mixed_hbm)
    def keep_term(ref, part, term):
        for b in range(4):
            k = lax.rem(b + 4 - x, 4)
            rows = slice(b * LANES, (b + 1) * LANES)
            ref[k, 2 * part] = term[rows, :LANES]
            ref[k, 2 * part + 1] = term[rows, LANES:]

    for g, ref in ((1 - group, send), (group, keep)):
        for part in range(3):
            chans = pl.ds(pl.multiple_of(g * 768 + part * 256, 256), 256)
            keep_term(ref, part, dot_t(nrm_t[...], qg_t[chans, :]).astype(BF))
        cols = pl.ds(pl.multiple_of(g * 256, 256), 256)
        keep_term(ref, 3, dot(ctx_t[...], gout[:, cols]).astype(BF))
    for copy in copies[-2:]:
        copy.wait()


def pair_kernel(keep_ref, theirs_ref, *out_refs):
    for k in range(4):
        out_refs[k][...] = (keep_ref[k].astype(F32) + theirs_ref[k].astype(F32)).astype(BF)


def total_kernel(factor, terms_ref, out_ref):
    total = terms_ref[0].astype(F32)
    for i in range(1, 64):
        total = total + terms_ref[i].astype(F32)
    out_ref[...] = jnp.broadcast_to((total * factor)[None], out_ref.shape)


def columns_kernel(blocks_ref, qkv_ref, out_ref):
    for y in range(8):
        for core in range(2):
            first = y // 2 * WIDTH + core * 256 + y % 2 * LANES
            block = blocks_ref[2 * y + core]
            if first < 3 * WIDTH:
                qkv_ref[:, first : first + LANES] = block
            else:
                out_ref[:, first - 3 * WIDTH : first - 3 * WIDTH + LANES] = block


def unpack_kernel(slot_ref, back_ref, out_ref):
    slot = slot_ref[0:1, :]
    row = iota((LANES, POINTS), 0)
    digits = jnp.where(row == 0, slot // 32, jnp.where(row == 1, slot % 32, 0))
    eye = onehot(iota((POINTS, POINTS), 0) == iota((POINTS, POINTS), 1))
    cols = dot_t(eye, digits.astype(F32).astype(BF))
    slot_col = (cols[:, 0:1] * 32.0 + cols[:, 1:2]).astype(jnp.int32)
    take = onehot(iota((POINTS, SLOTS), 1) == slot_col)
    for c in range(0, 4, 2):
        out_ref[:, c * LANES : (c + 2) * LANES] = dot(take, slot_rows(back_ref, c)).astype(BF)


VMEM = pl.BlockSpec(memory_space=pltpu.VMEM)
SMEM = pl.BlockSpec(memory_space=pltpu.SMEM)
ANY = pl.BlockSpec(memory_space=pl.ANY)
HBM = pl.BlockSpec(memory_space=pltpu.HBM)


def params(mib):
    return pltpu.CompilerParams(vmem_limit_bytes=mib * 1024 * 1024)


def exchange(array, axes):
    return lax.all_to_all(array, axes, split_axis=0, concat_axis=0, tiled=True)


def cost(flops, size):
    return pl.CostEstimate(flops=flops, bytes_accessed=size, transcendentals=0)


def shift(array, axis, size, by):
    return lax.ppermute(array, axis, [(i, (i + by) % size) for i in range(size)])


def local(feats, hilbert_pos, w_qkv, w_out, grad_out):
    core, x = lax.axis_index("core"), lax.axis_index("x")
    at = jnp.stack([core, x]).astype(jnp.int32)
    pieces = [w_qkv[:, :WIDTH], w_qkv[:, WIDTH : 2 * WIDTH], w_qkv[:, 2 * WIDTH :], w_out]
    by_z = jnp.concatenate(
        [jnp.where(core == 0, piece[:, :256], piece[:, 256:]) for piece in pieces], axis=1
    )[None]
    by_z = exchange(jnp.broadcast_to(by_z, (8, 16, W_COLS)), "z").reshape(128, W_COLS)
    send, slot = pl.pallas_call(
        pack_kernel,
        out_shape=(
            jax.ShapeDtypeStruct((SHARDS, SEND_ROWS, LANES), BF),
            jax.ShapeDtypeStruct((8, POINTS), jnp.int32),
        ),
        in_specs=[VMEM, VMEM],
        out_specs=(VMEM, VMEM),
        compiler_params=params(32),
        cost_estimate=cost(10**9, 4 << 20),
        name="pack",
    )(hilbert_pos, feats[0])
    recv = exchange(send, SEQ)
    mine = [by_z] + [shift(by_z, "x", 4, k) for k in X_SHIFTS[1:]]
    other = shift(jnp.stack(mine), "core", 2, 1)
    wgrad = jax.ShapeDtypeStruct((4, 8, LANES, LANES), BF)
    out_shape = (
        jax.ShapeDtypeStruct((POINTS, WIDTH), BF),
        wgrad,
        wgrad,
        jax.ShapeDtypeStruct((SHARDS, FEAT_ROWS, LANES), BF),
    )
    hilbert, normed, digits = pl.pallas_call(
        arrive_kernel,
        out_shape=(
            jax.ShapeDtypeStruct((POINTS, WIDTH), BF),
            jax.ShapeDtypeStruct((POINTS, WIDTH), BF),
            jax.ShapeDtypeStruct((SHARDS, LANES), BF),
        ),
        in_specs=[VMEM],
        out_specs=(VMEM,) * 3,
        compiler_params=params(32),
        cost_estimate=cost(2 * 10**9, 4 << 20),
        name="arrive",
    )(recv)
    mixed, keep, give, back = pl.pallas_call(
        block_kernel,
        out_shape=out_shape,
        in_specs=[SMEM] + [VMEM] * 8 + [HBM],
        out_specs=(ANY, VMEM, VMEM, ANY),
        scratch_shapes=[
            pltpu.VMEM((2, WIDTH, W_COLS), BF),
            pltpu.VMEM((POINTS, WIDTH), BF),
            pltpu.VMEM((POINTS, WIDTH), BF),
            pltpu.VMEM((SHARDS, FEAT_ROWS, LANES), BF),
            pltpu.VMEM((WIDTH, POINTS), BF),
            pltpu.VMEM((POINTS, 3 * WIDTH), BF),
            pltpu.VMEM((POINTS, WIDTH), BF),
            pltpu.VMEM((WIDTH, POINTS), BF),
            pltpu.VMEM((3 * WIDTH, POINTS), BF),
            pltpu.VMEM((2, 2, 8 * PATCH, PATCH), F32),
            pltpu.SemaphoreType.DMA((11,)),
        ],
        compiler_params=params(50),
        cost_estimate=cost(10**10, 8 << 20),
        name="block",
    )(at, hilbert, normed, digits, *mine, other, grad_out[0])
    theirs = shift(give, "core", 2, 1)
    pair = pl.pallas_call(
        pair_kernel,
        out_shape=(jax.ShapeDtypeStruct((8, LANES, LANES), BF),) * 4,
        in_specs=[VMEM, VMEM],
        out_specs=(VMEM,) * 4,
        compiler_params=params(32),
        cost_estimate=cost(10**6, 3 << 20),
        name="pair",
    )(keep, theirs)
    returned = exchange(back, SEQ)
    by_x = [pair[0]] + [shift(pair[k], "x", 4, k) for k in (2, 3, 1)]
    *by_x, returned = lax.optimization_barrier((*by_x, returned))
    share = sum(term.astype(F32) for term in by_x).astype(BF)
    by_seq = exchange(share.reshape(64, WIDTH // SHARDS, LANES), ("y", "z"))
    factor = 1.0 / math.sqrt(16 * POINTS * SHARDS)
    total = pl.pallas_call(
        functools.partial(total_kernel, factor),
        out_shape=jax.ShapeDtypeStruct((16, WIDTH // SHARDS, LANES), F32),
        in_specs=[VMEM],
        out_specs=VMEM,
        compiler_params=params(16),
        cost_estimate=cost(10**6, 1 << 18),
        name="total",
    )(by_seq)
    whole = exchange(total, BATCH)
    qkv_wgrad, out_wgrad = pl.pallas_call(
        columns_kernel,
        out_shape=(
            jax.ShapeDtypeStruct((WIDTH // SHARDS, 3 * WIDTH), F32),
            jax.ShapeDtypeStruct((WIDTH // SHARDS, WIDTH), F32),
        ),
        in_specs=[VMEM],
        out_specs=(VMEM, VMEM),
        compiler_params=params(32),
        cost_estimate=cost(10**6, 1 << 18),
        name="columns",
    )(whole)
    feat_grad = pl.pallas_call(
        unpack_kernel,
        out_shape=jax.ShapeDtypeStruct((POINTS, WIDTH), BF),
        in_specs=[VMEM, VMEM],
        out_specs=VMEM,
        compiler_params=params(32),
        cost_estimate=cost(10**9, 4 << 20),
        name="unpack",
    )(slot, returned)
    return (mixed[None], feat_grad[None], qkv_wgrad, out_wgrad)


def solution(mesh):
    mesh = Mesh(mesh.devices.reshape(4, 8, 8, 2), ("x", "z", "y", "core"))
    rows = P(BATCH, SEQ, None)
    return jax.shard_map(
        local,
        mesh=mesh,
        in_specs=(rows, P(BATCH, SEQ), P(SEQ, None), P(SEQ, None), rows),
        out_specs=(rows, rows, P(SEQ, None), P(SEQ, None)),
        check_vma=False,
    )
```

```python
import functools
import math

import jax
import jax.numpy as jnp
from jax import lax
from jax.experimental import pallas as pl
from jax.experimental.pallas import tpu as pltpu
from jax.sharding import Mesh
from jax.sharding import PartitionSpec as P

HEADS = 32
HEAD_CHANNELS = 16
PATCH = 128
WIDTH = 512
POINTS = 512
SHARDS = 32
CAP = 32
SLOTS = SHARDS * CAP
LANES = 128
EPS = 1e-05
SCALE = HEAD_CHANNELS ** (-0.5)

BF = jnp.bfloat16
F32 = jnp.float32
SEQ = ("x", "z")
BATCH = ("y", "core")

FEAT_ROWS = 4 * CAP
SEND_ROWS = FEAT_ROWS + 16
W_COLS = 1024
X_SHIFTS = (0, 1, 3, 2)


def iota(shape, dim):
    return lax.broadcasted_iota(jnp.int32, shape, dim)


def onehot(condition):
    return jnp.where(condition, 1.0, 0.0).astype(BF)


def dot(left, right):
    return jnp.dot(left, right, preferred_element_type=F32)


def dot_t(left, right):
    return lax.dot_general(left, right, (((1,), (1,)), ((), ())), preferred_element_type=F32)


def pack_kernel(pos_ref, feats_ref, out_ref, slot_ref):
    target = pos_ref[...]
    owner = target // POINTS
    place = target % POINTS + 1
    mine = iota((SHARDS, POINTS), 0) == owner
    mine_b = onehot(mine)
    before = onehot(iota((POINTS, POINTS), 0) < iota((POINTS, POINTS), 1))
    ranks = dot(mine_b, before)
    rank = jnp.sum(jnp.where(mine, ranks, 0.0), axis=0, keepdims=True).astype(jnp.int32)
    slot = owner * CAP + rank
    slot_ref[...] = jnp.broadcast_to(slot, slot_ref.shape)
    place_of = onehot(iota((SLOTS, POINTS), 0) == slot)
    lane = iota((LANES, POINTS), 0)
    digits = jnp.where(lane == rank, place // 32, 0) + jnp.where(lane == rank + CAP, place % 32, 0)
    pos = dot_t(mine_b, digits.astype(F32).astype(BF)).astype(BF)
    out_ref[:, FEAT_ROWS:SEND_ROWS, :] = jnp.broadcast_to(pos[:, None, :], (SHARDS, 16, LANES))
    for c in range(0, 4, 2):
        rows = dot(place_of, feats_ref[:, c * LANES : (c + 2) * LANES]).astype(BF)
        for b in range(2):
            block = rows[:, b * LANES : (b + 1) * LANES]
            out_ref[:, (c + b) * CAP : (c + b + 1) * CAP, :] = block.reshape(SHARDS, CAP, LANES)


def positions(recv_ref):
    return recv_ref[:, FEAT_ROWS:SEND_ROWS, :][:, 0, :]


def slot_rows(ref, c):
    blocks = [
        ref[:, b * CAP : (b + 1) * CAP, :].reshape(SLOTS, LANES) for b in (c, c + 1)
    ]
    return jnp.concatenate(blocks, axis=1)


def arrivals(digits):
    lane, slot = iota((LANES, SLOTS), 0), iota((LANES, SLOTS), 1) % CAP
    spread = jnp.where(lane == slot, 32.0, jnp.where(lane == slot + CAP, 1.0, 0.0)).astype(BF)
    each = dot(digits, spread)
    source = iota((SHARDS, SLOTS), 0) == iota((SHARDS, SLOTS), 1) // CAP
    place = jnp.sum(jnp.where(source, each, 0.0), axis=0, keepdims=True).astype(jnp.int32) - 1
    return onehot(iota((POINTS, SLOTS), 0) == place)


def departures(digits):
    source = onehot(iota((SLOTS, SHARDS), 0) // CAP == iota((SLOTS, SHARDS), 1))
    each = dot(source, digits)
    slot, lane = iota((SLOTS, LANES), 0) % CAP, iota((SLOTS, LANES), 1)
    weight = jnp.where(lane == slot, 32.0, jnp.where(lane == slot + CAP, 1.0, 0.0))
    place = jnp.sum(each * weight, axis=1, keepdims=True).astype(jnp.int32) - 1
    return onehot(iota((SLOTS, POINTS), 1) == place)


def arrive_kernel(recv, hil, nrm, digits_ref):
    digits = positions(recv)
    digits_ref[...] = digits
    arrive = arrivals(digits)
    rows = []
    for c in range(0, 4, 2):
        rows.append(dot(arrive, slot_rows(recv, c)))
        hil[:, c * LANES : (c + 2) * LANES] = rows[-1].astype(BF)
    rows = jnp.concatenate(rows, axis=1)
    centred = rows - jnp.mean(rows, axis=-1, keepdims=True)
    inv_scale = lax.rsqrt(jnp.mean(centred * centred, axis=-1, keepdims=True) + EPS)
    nrm[...] = (centred * inv_scale).astype(BF)


def block_kernel(
    at_ref,
    nrm,
    mine0_ref,
    mine1_ref,
    mine2_ref,
    mine3_ref,
    other_ref,
    gout_hbm,
    keep,
    send,
    w,
    ctx_t,
    qg_t,
    gout,
    nrm_t,
    qkv,
    cgrad,
    sd,
    sems,
):
    group, x = at_ref[0], at_ref[1]
    copies = []

    def start(source, target):
        copy = pltpu.make_async_copy(source, target, sems.at[len(copies)])
        copy.start()
        copies.append(copy)
        return copy

    w_copies = []
    for k, mine in enumerate((mine0_ref, mine1_ref, mine2_ref, mine3_ref)):
        rows = pl.ds(pl.multiple_of(lax.rem(x + 4 - X_SHIFTS[k], 4) * 128, 128), 128)
        w_copies.append(start(mine, w.at[group, rows, :]))
        w_copies.append(start(other_ref.at[k], w.at[1 - group, rows, :]))
    gout_copy = start(gout_hbm, gout)
    nrm_t[...] = nrm[...].T
    normed = nrm[...]
    for copy in w_copies:
        copy.wait()
    for g in range(2):
        for part in range(3):
            cols = slice(part * 256, (part + 1) * 256)
            at = slice(g * 768 + part * 256, g * 768 + (part + 1) * 256)
            qkv[:, at] = dot(normed, w[g, :, cols]).astype(BF)
    gout_copy.wait()
    cgrad[...] = (
        dot_t(gout[:, :256], w[0, :, 768:]) + dot_t(gout[:, 256:], w[1, :, 768:])
    ).astype(BF)

    by_lane = iota((1, LANES), 1) // HEAD_CHANNELS
    by_row = iota((LANES, 1), 0) // HEAD_CHANNELS
    lane_heads = [jnp.where(by_lane == h, 1.0, 0.0).astype(BF) for h in range(8)]
    row_heads = [jnp.where(by_row == h, 1.0, 0.0).astype(BF) for h in range(8)]

    def stack(array):
        return jnp.concatenate([array * head for head in lane_heads], axis=0)

    def spread(array):
        return jnp.concatenate([array * head for head in row_heads], axis=1)

    def places(u):
        p = u // 4
        o = u % 4
        pts = pl.ds(pl.multiple_of(p * PATCH, PATCH), PATCH)
        first = (o // 2) * 768 + (o % 2) * LANES
        block = lambda part: pl.ds(pl.multiple_of(first + part * 256, LANES), LANES)
        whole = pl.ds(pl.multiple_of(o * LANES, LANES), LANES)
        return pts, block, whole

    def scores_of(u, slot):
        pts, block, whole = places(u)
        sd[slot, 0] = dot_t(stack(qkv[pts, block(1)]), qkv[pts, block(0)] * BF(SCALE))
        sd[slot, 1] = dot_t(stack(qkv[pts, block(2)]), cgrad[pts, whole])

    def unit(u, slot):
        pts, block, whole = places(u)
        qs = qkv[pts, block(0)] * BF(SCALE)
        k = qkv[pts, block(1)]
        v = qkv[pts, block(2)]
        dc = cgrad[pts, whole]
        probs_b, score_grads = [], []
        for h in range(8):
            scores = sd[slot, 0, h * PATCH : (h + 1) * PATCH, :]
            prob_grad = sd[slot, 1, h * PATCH : (h + 1) * PATCH, :]
            exps = jnp.exp(scores - jnp.max(scores, axis=0, keepdims=True))
            probs = exps * (1.0 / jnp.sum(exps, axis=0, keepdims=True))
            total = jnp.sum(probs * prob_grad, axis=0, keepdims=True)
            probs_b.append(probs.astype(BF))
            score_grads.append((probs * (prob_grad - total)).astype(BF))
        rows_p, cols_p = jnp.concatenate(probs_b, axis=0), jnp.concatenate(probs_b, axis=1)
        rows_s, cols_s = jnp.concatenate(score_grads, axis=0), jnp.concatenate(score_grads, axis=1)
        both = dot(
            jnp.concatenate([spread(v.T), spread((k * BF(SCALE)).T)], axis=0),
            jnp.concatenate([rows_p, rows_s], axis=1),
        ).astype(BF)
        ctx_t[whole, pts] = both[:LANES, :PATCH]
        qg_t[block(0), pts] = both[LANES:, PATCH:]
        both = dot(
            jnp.concatenate([cols_s, cols_p], axis=0),
            jnp.concatenate([stack(qs), stack(dc)], axis=1),
        ).astype(BF)
        qg_t[block(1), pts] = both[:PATCH, :LANES].T
        qg_t[block(2), pts] = both[PATCH:, LANES:].T

    def two_units(t, carry):
        scores_of(2 * t + 1, 1)
        unit(2 * t, 0)
        scores_of(jnp.minimum(2 * t + 2, 15), 0)
        unit(2 * t + 1, 1)
        return carry

    scores_of(0, 0)
    lax.fori_loop(0, 8, two_units, 0, unroll=4)

    def keep_term(ref, part, term):
        for b in range(4):
            k = lax.rem(b + 4 - x, 4)
            rows = slice(b * LANES, (b + 1) * LANES)
            ref[k, 2 * part] = term[rows, :LANES]
            ref[k, 2 * part + 1] = term[rows, LANES:]

    for g, ref in ((1 - group, send), (group, keep)):
        for part in range(3):
            chans = pl.ds(pl.multiple_of(g * 768 + part * 256, 256), 256)
            keep_term(ref, part, dot_t(nrm_t[...], qg_t[chans, :]).astype(BF))
        cols = pl.ds(pl.multiple_of(g * 256, 256), 256)
        keep_term(ref, 3, dot(ctx_t[...], gout[:, cols]).astype(BF))

def finish_kernel(hil, digits_ref, w, ctx_t, qg_t, gout_hbm, mixed_hbm, back, gout, mixed, sems):
    gout_copy = pltpu.make_async_copy(gout_hbm, gout, sems.at[0])
    gout_copy.start()
    context = ctx_t[...].T
    for g in range(2):
        cols = slice(g * 256, (g + 1) * 256)
        mixed[:, cols] = (hil[:, cols].astype(F32) + dot(context, w[g, :, 768:])).astype(BF)
    mixed_copy = pltpu.make_async_copy(mixed, mixed_hbm, sems.at[1])
    mixed_copy.start()
    rows = hil[...].astype(F32)
    centred = rows - jnp.mean(rows, axis=-1, keepdims=True)
    inv_scale = lax.rsqrt(jnp.mean(centred * centred, axis=-1, keepdims=True) + EPS)
    xhat = centred * inv_scale
    ngrad = (dot(w[0, :, :768], qg_t[:768, :]) + dot(w[1, :, :768], qg_t[768:, :])).T
    cent = ngrad - jnp.mean(ngrad, axis=-1, keepdims=True)
    cent = cent - xhat * jnp.mean(ngrad * xhat, axis=-1, keepdims=True)
    gout_copy.wait()
    hgrad = (gout[...].astype(F32) + inv_scale * cent).astype(BF)
    leave = departures(digits_ref[...])
    for c in range(0, 4, 2):
        out = dot(leave, hgrad[:, c * LANES : (c + 2) * LANES]).astype(BF)
        back[:, :, c * LANES : (c + 2) * LANES] = out.reshape(SHARDS, CAP, 2 * LANES)
    mixed_copy.wait()


def pair_kernel(keep_ref, theirs_ref, *out_refs):
    for k in range(4):
        out_refs[k][...] = (keep_ref[k].astype(F32) + theirs_ref[k].astype(F32)).astype(BF)


def total_kernel(factor, terms_ref, out_ref):
    total = terms_ref[0].astype(F32)
    for i in range(1, 64):
        total = total + terms_ref[i].astype(F32)
    out_ref[...] = jnp.broadcast_to((total * factor).astype(BF)[None], out_ref.shape)


def columns_kernel(blocks_ref, qkv_ref, out_ref):
    for y in range(8):
        for core in range(2):
            first = y // 2 * WIDTH + core * 256 + y % 2 * LANES
            block = blocks_ref[2 * y + core].astype(F32)
            if first < 3 * WIDTH:
                qkv_ref[:, first : first + LANES] = block
            else:
                out_ref[:, first - 3 * WIDTH : first - 3 * WIDTH + LANES] = block


def unpack_kernel(slot_ref, back_ref, out_ref):
    slot = slot_ref[0:1, :]
    row = iota((LANES, POINTS), 0)
    digits = jnp.where(row == 0, slot // 32, jnp.where(row == 1, slot % 32, 0))
    eye = onehot(iota((POINTS, POINTS), 0) == iota((POINTS, POINTS), 1))
    cols = dot_t(eye, digits.astype(F32).astype(BF))
    slot_col = (cols[:, 0:1] * 32.0 + cols[:, 1:2]).astype(jnp.int32)
    take = onehot(iota((POINTS, SLOTS), 1) == slot_col)
    for c in range(0, 4, 2):
        cols = slice(c * LANES, (c + 2) * LANES)
        got = back_ref[:, :, cols].reshape(SLOTS, 2 * LANES)
        out_ref[:, cols] = dot(take, got).astype(BF)


VMEM = pl.BlockSpec(memory_space=pltpu.VMEM)
SMEM = pl.BlockSpec(memory_space=pltpu.SMEM)
ANY = pl.BlockSpec(memory_space=pl.ANY)
HBM = pl.BlockSpec(memory_space=pltpu.HBM)


def params(mib):
    return pltpu.CompilerParams(vmem_limit_bytes=mib * 1024 * 1024)


def exchange(array, axes):
    return lax.all_to_all(array, axes, split_axis=0, concat_axis=0, tiled=True)


def cost(flops, size):
    return pl.CostEstimate(flops=flops, bytes_accessed=size, transcendentals=0)


def shift(array, axis, size, by):
    return lax.ppermute(array, axis, [(i, (i + by) % size) for i in range(size)])


def local(feats, hilbert_pos, w_qkv, w_out, grad_out):
    core, x = lax.axis_index("core"), lax.axis_index("x")
    at = jnp.stack([core, x]).astype(jnp.int32)
    pieces = [w_qkv[:, :WIDTH], w_qkv[:, WIDTH : 2 * WIDTH], w_qkv[:, 2 * WIDTH :], w_out]
    by_z = jnp.concatenate(
        [jnp.where(core == 0, piece[:, :256], piece[:, 256:]) for piece in pieces], axis=1
    )[None]
    by_z = exchange(jnp.broadcast_to(by_z, (8, 16, W_COLS)), "z").reshape(128, W_COLS)
    send, slot = pl.pallas_call(
        pack_kernel,
        out_shape=(
            jax.ShapeDtypeStruct((SHARDS, SEND_ROWS, LANES), BF),
            jax.ShapeDtypeStruct((8, POINTS), jnp.int32),
        ),
        in_specs=[VMEM, VMEM],
        out_specs=(VMEM, VMEM),
        compiler_params=params(12),
        cost_estimate=cost(10**9, 4 << 20),
        name="pack",
    )(hilbert_pos, feats[0])
    recv = exchange(send, SEQ)
    mine = [by_z] + [shift(by_z, "x", 4, k) for k in X_SHIFTS[1:]]
    other = shift(jnp.stack(mine), "core", 2, 1)
    wgrad = jax.ShapeDtypeStruct((4, 8, LANES, LANES), BF)
    hilbert, normed, digits = pl.pallas_call(
        arrive_kernel,
        out_shape=(
            jax.ShapeDtypeStruct((POINTS, WIDTH), BF),
            jax.ShapeDtypeStruct((POINTS, WIDTH), BF),
            jax.ShapeDtypeStruct((SHARDS, LANES), BF),
        ),
        in_specs=[VMEM],
        out_specs=(VMEM,) * 3,
        compiler_params=params(12),
        cost_estimate=cost(2 * 10**9, 4 << 20),
        name="arrive",
    )(recv)
    keep, give, weights, context_t, qkv_grad_t = pl.pallas_call(
        block_kernel,
        out_shape=(
            wgrad,
            wgrad,
            jax.ShapeDtypeStruct((2, WIDTH, W_COLS), BF),
            jax.ShapeDtypeStruct((WIDTH, POINTS), BF),
            jax.ShapeDtypeStruct((3 * WIDTH, POINTS), BF),
        ),
        in_specs=[SMEM] + [VMEM] * 6 + [HBM],
        out_specs=(VMEM,) * 5,
        scratch_shapes=[
            pltpu.VMEM((POINTS, WIDTH), BF),
            pltpu.VMEM((WIDTH, POINTS), BF),
            pltpu.VMEM((POINTS, 3 * WIDTH), BF),
            pltpu.VMEM((POINTS, WIDTH), BF),
            pltpu.VMEM((2, 2, 8 * PATCH, PATCH), F32),
            pltpu.SemaphoreType.DMA((9,)),
        ],
        compiler_params=params(24),
        cost_estimate=cost(10**10, 8 << 20),
        name="block",
    )(at, normed, *mine, other, grad_out[0])
    mixed, back = pl.pallas_call(
        finish_kernel,
        out_shape=(
            jax.ShapeDtypeStruct((POINTS, WIDTH), BF),
            jax.ShapeDtypeStruct((SHARDS, CAP, WIDTH), BF),
        ),
        in_specs=[VMEM] * 5 + [HBM],
        out_specs=(ANY, VMEM),
        scratch_shapes=[
            pltpu.VMEM((POINTS, WIDTH), BF),
            pltpu.VMEM((POINTS, WIDTH), BF),
            pltpu.SemaphoreType.DMA((2,)),
        ],
        compiler_params=params(12),
        cost_estimate=cost(4 * 10**9, 8 << 20),
        name="finish",
    )(hilbert, digits, weights, context_t, qkv_grad_t, grad_out[0])
    theirs = shift(give, "core", 2, 1)
    pair = pl.pallas_call(
        pair_kernel,
        out_shape=(jax.ShapeDtypeStruct((8, LANES, LANES), BF),) * 4,
        in_specs=[VMEM, VMEM],
        out_specs=(VMEM,) * 4,
        compiler_params=params(12),
        cost_estimate=cost(10**6, 3 << 20),
        name="pair",
    )(keep, theirs)
    *pair, back = lax.optimization_barrier((*pair, back))
    returned = exchange(back, SEQ)
    by_x = [pair[0]] + [shift(pair[k], "x", 4, k) for k in (2, 3, 1)]
    *by_x, returned = lax.optimization_barrier((*by_x, returned))
    share = sum(term.astype(F32) for term in by_x).astype(BF)
    by_seq = exchange(share.reshape(64, WIDTH // SHARDS, LANES), ("y", "z"))
    factor = 1.0 / math.sqrt(16 * POINTS * SHARDS)
    total = pl.pallas_call(
        functools.partial(total_kernel, factor),
        out_shape=jax.ShapeDtypeStruct((16, WIDTH // SHARDS, LANES), BF),
        in_specs=[VMEM],
        out_specs=VMEM,
        compiler_params=params(16),
        cost_estimate=cost(10**6, 1 << 18),
        name="total",
    )(by_seq)
    whole = exchange(total, BATCH)
    qkv_wgrad, out_wgrad = pl.pallas_call(
        columns_kernel,
        out_shape=(
            jax.ShapeDtypeStruct((WIDTH // SHARDS, 3 * WIDTH), F32),
            jax.ShapeDtypeStruct((WIDTH // SHARDS, WIDTH), F32),
        ),
        in_specs=[VMEM],
        out_specs=(VMEM, VMEM),
        compiler_params=params(12),
        cost_estimate=cost(10**6, 1 << 18),
        name="columns",
    )(whole)
    feat_grad = pl.pallas_call(
        unpack_kernel,
        out_shape=jax.ShapeDtypeStruct((POINTS, WIDTH), BF),
        in_specs=[VMEM, VMEM],
        out_specs=VMEM,
        compiler_params=params(12),
        cost_estimate=cost(10**9, 4 << 20),
        name="unpack",
    )(slot, returned)
    return (mixed[None], feat_grad[None], qkv_wgrad, out_wgrad)


def solution(mesh):
    mesh = Mesh(mesh.devices.reshape(4, 8, 8, 2), ("x", "z", "y", "core"))
    rows = P(BATCH, SEQ, None)
    return jax.shard_map(
        local,
        mesh=mesh,
        in_specs=(rows, P(BATCH, SEQ), P(SEQ, None), P(SEQ, None), rows),
        out_specs=(rows, rows, P(SEQ, None), P(SEQ, None)),
        check_vma=False,
    )
```

```python
import functools
import math

import jax
import jax.numpy as jnp
from jax import lax
from jax.experimental import pallas as pl
from jax.experimental.pallas import tpu as pltpu
from jax.sharding import Mesh
from jax.sharding import PartitionSpec as P

HEADS = 32
HEAD_CHANNELS = 16
PATCH = 128
WIDTH = 512
POINTS = 512
SHARDS = 32
CAP = 32
SLOTS = SHARDS * CAP
LANES = 128
EPS = 1e-05
SCALE = HEAD_CHANNELS ** (-0.5)

BF = jnp.bfloat16
F32 = jnp.float32
SEQ = ("x", "z")
BATCH = ("y", "core")

FEAT_ROWS = 4 * CAP
SEND_ROWS = FEAT_ROWS + 16
W_COLS = 1024
X_SHIFTS = (0, 1, 3, 2)


def iota(shape, dim):
    return lax.broadcasted_iota(jnp.int32, shape, dim)


def onehot(condition):
    return jnp.where(condition, 1.0, 0.0).astype(BF)


def dot(left, right):
    return jnp.dot(left, right, preferred_element_type=F32)


def dot_t(left, right):
    return lax.dot_general(left, right, (((1,), (1,)), ((), ())), preferred_element_type=F32)


def pack_kernel(pos_ref, feats_ref, out_ref, slot_ref):
    target = pos_ref[...]
    owner = target // POINTS
    place = target % POINTS + 1
    mine = iota((SHARDS, POINTS), 0) == owner
    mine_b = onehot(mine)
    before = onehot(iota((POINTS, POINTS), 0) < iota((POINTS, POINTS), 1))
    ranks = dot(mine_b, before)
    rank = jnp.sum(jnp.where(mine, ranks, 0.0), axis=0, keepdims=True).astype(jnp.int32)
    slot = owner * CAP + rank
    slot_ref[...] = jnp.broadcast_to(slot, slot_ref.shape)
    place_of = onehot(iota((SLOTS, POINTS), 0) == slot)
    lane = iota((LANES, POINTS), 0)
    digits = jnp.where(lane == rank, place // 32, 0) + jnp.where(lane == rank + CAP, place % 32, 0)
    pos = dot_t(mine_b, digits.astype(F32).astype(BF)).astype(BF)
    out_ref[:, FEAT_ROWS:SEND_ROWS, :] = jnp.broadcast_to(pos[:, None, :], (SHARDS, 16, LANES))
    for c in range(0, 4, 2):
        rows = dot(place_of, feats_ref[:, c * LANES : (c + 2) * LANES]).astype(BF)
        for b in range(2):
            block = rows[:, b * LANES : (b + 1) * LANES]
            out_ref[:, (c + b) * CAP : (c + b + 1) * CAP, :] = block.reshape(SHARDS, CAP, LANES)


def positions(recv_ref):
    return recv_ref[:, FEAT_ROWS:SEND_ROWS, :][:, 0, :]


def slot_rows(ref, c):
    blocks = [
        ref[:, b * CAP : (b + 1) * CAP, :].reshape(SLOTS, LANES) for b in (c, c + 1)
    ]
    return jnp.concatenate(blocks, axis=1)


def arrivals(digits):
    lane, slot = iota((LANES, SLOTS), 0), iota((LANES, SLOTS), 1) % CAP
    spread = jnp.where(lane == slot, 32.0, jnp.where(lane == slot + CAP, 1.0, 0.0)).astype(BF)
    each = dot(digits, spread)
    source = iota((SHARDS, SLOTS), 0) == iota((SHARDS, SLOTS), 1) // CAP
    place = jnp.sum(jnp.where(source, each, 0.0), axis=0, keepdims=True).astype(jnp.int32) - 1
    return onehot(iota((POINTS, SLOTS), 0) == place)


def departures(digits):
    source = onehot(iota((SLOTS, SHARDS), 0) // CAP == iota((SLOTS, SHARDS), 1))
    each = dot(source, digits)
    slot, lane = iota((SLOTS, LANES), 0) % CAP, iota((SLOTS, LANES), 1)
    weight = jnp.where(lane == slot, 32.0, jnp.where(lane == slot + CAP, 1.0, 0.0))
    place = jnp.sum(each * weight, axis=1, keepdims=True).astype(jnp.int32) - 1
    return onehot(iota((SLOTS, POINTS), 1) == place)


def arrive_kernel(recv, hil, nrm, digits_ref):
    digits = positions(recv)
    digits_ref[...] = digits
    arrive = arrivals(digits)
    rows = []
    for c in range(0, 4, 2):
        rows.append(dot(arrive, slot_rows(recv, c)))
        hil[:, c * LANES : (c + 2) * LANES] = rows[-1].astype(BF)
    rows = jnp.concatenate(rows, axis=1)
    centred = rows - jnp.mean(rows, axis=-1, keepdims=True)
    inv_scale = lax.rsqrt(jnp.mean(centred * centred, axis=-1, keepdims=True) + EPS)
    nrm[...] = (centred * inv_scale).astype(BF)


def block_kernel(
    at_ref,
    nrm,
    mine0_ref,
    mine1_ref,
    mine2_ref,
    mine3_ref,
    other_ref,
    gout_hbm,
    keep,
    send,
    w,
    ctx_t,
    qkv_grad,
    gout,
    nrm_t,
    qkv,
    cgrad,
    sd,
    sems,
):
    group, x = at_ref[0], at_ref[1]
    copies = []

    def start(source, target):
        copy = pltpu.make_async_copy(source, target, sems.at[len(copies)])
        copy.start()
        copies.append(copy)
        return copy

    w_copies = []
    for k, mine in enumerate((mine0_ref, mine1_ref, mine2_ref, mine3_ref)):
        rows = pl.ds(pl.multiple_of(lax.rem(x + 4 - X_SHIFTS[k], 4) * 128, 128), 128)
        w_copies.append(start(mine, w.at[group, rows, :]))
        w_copies.append(start(other_ref.at[k], w.at[1 - group, rows, :]))
    gout_copy = start(gout_hbm, gout)
    nrm_t[...] = nrm[...].T
    normed = nrm[...]
    for copy in w_copies:
        copy.wait()
    for g in range(2):
        for part in range(3):
            cols = slice(part * 256, (part + 1) * 256)
            at = slice(g * 768 + part * 256, g * 768 + (part + 1) * 256)
            qkv[:, at] = dot(normed, w[g, :, cols]).astype(BF)
    gout_copy.wait()
    cgrad[...] = (
        dot_t(gout[:, :256], w[0, :, 768:]) + dot_t(gout[:, 256:], w[1, :, 768:])
    ).astype(BF)

    by_lane = iota((1, LANES), 1) // HEAD_CHANNELS
    by_row = iota((LANES, 1), 0) // HEAD_CHANNELS
    lane_heads = [jnp.where(by_lane == h, 1.0, 0.0).astype(BF) for h in range(8)]
    row_heads = [jnp.where(by_row == h, 1.0, 0.0).astype(BF) for h in range(8)]

    def stack(array):
        return jnp.concatenate([array * head for head in lane_heads], axis=0)

    def spread(array):
        return jnp.concatenate([array * head for head in row_heads], axis=1)

    def places(u):
        p = u // 4
        o = u % 4
        pts = pl.ds(pl.multiple_of(p * PATCH, PATCH), PATCH)
        first = (o // 2) * 768 + (o % 2) * LANES
        block = lambda part: pl.ds(pl.multiple_of(first + part * 256, LANES), LANES)
        whole = pl.ds(pl.multiple_of(o * LANES, LANES), LANES)
        return pts, block, whole

    def scores_of(u, slot):
        pts, block, whole = places(u)
        sd[slot, 0] = dot_t(stack(qkv[pts, block(1)]), qkv[pts, block(0)] * BF(SCALE))
        sd[slot, 1] = dot_t(stack(qkv[pts, block(2)]), cgrad[pts, whole])

    def unit(u, slot):
        pts, block, whole = places(u)
        qs = qkv[pts, block(0)] * BF(SCALE)
        k = qkv[pts, block(1)]
        v = qkv[pts, block(2)]
        dc = cgrad[pts, whole]
        probs_b, score_grads = [], []
        for h in range(8):
            scores = sd[slot, 0, h * PATCH : (h + 1) * PATCH, :]
            prob_grad = sd[slot, 1, h * PATCH : (h + 1) * PATCH, :]
            exps = jnp.exp(scores - jnp.max(scores, axis=0, keepdims=True))
            probs = exps * (1.0 / jnp.sum(exps, axis=0, keepdims=True))
            total = jnp.sum(probs * prob_grad, axis=0, keepdims=True)
            probs_b.append(probs.astype(BF))
            score_grads.append((probs * (prob_grad - total)).astype(BF))
        rows_p, cols_p = jnp.concatenate(probs_b, axis=0), jnp.concatenate(probs_b, axis=1)
        rows_s, cols_s = jnp.concatenate(score_grads, axis=0), jnp.concatenate(score_grads, axis=1)
        both = dot(
            jnp.concatenate([spread(v.T), spread((k * BF(SCALE)).T)], axis=0),
            jnp.concatenate([rows_p, rows_s], axis=1),
        ).astype(BF)
        ctx_t[whole, pts] = both[:LANES, :PATCH]
        qkv_grad[pts, block(0)] = both[LANES:, PATCH:].T
        both = dot(
            jnp.concatenate([cols_s, cols_p], axis=0),
            jnp.concatenate([stack(qs), stack(dc)], axis=1),
        ).astype(BF)
        qkv_grad[pts, block(1)] = both[:PATCH, :LANES]
        qkv_grad[pts, block(2)] = both[PATCH:, LANES:]

    def two_units(t, carry):
        scores_of(2 * t + 1, 1)
        unit(2 * t, 0)
        scores_of(jnp.minimum(2 * t + 2, 15), 0)
        unit(2 * t + 1, 1)
        return carry

    scores_of(0, 0)
    lax.fori_loop(0, 8, two_units, 0, unroll=4)

    def keep_term(ref, part, term):
        for b in range(4):
            k = lax.rem(b + 4 - x, 4)
            rows = slice(b * LANES, (b + 1) * LANES)
            ref[k, 2 * part] = term[rows, :LANES]
            ref[k, 2 * part + 1] = term[rows, LANES:]

    for g, ref in ((1 - group, send), (group, keep)):
        for part in range(3):
            chans = pl.ds(pl.multiple_of(g * 768 + part * 256, 256), 256)
            keep_term(ref, part, dot(nrm_t[...], qkv_grad[:, chans]).astype(BF))
        cols = pl.ds(pl.multiple_of(g * 256, 256), 256)
        keep_term(ref, 3, dot(ctx_t[...], gout[:, cols]).astype(BF))

def finish_kernel(hil, digits_ref, w, ctx_t, qkv_grad, gout_hbm, mixed_hbm, back, gout, mixed, sems):
    gout_copy = pltpu.make_async_copy(gout_hbm, gout, sems.at[0])
    gout_copy.start()
    context = ctx_t[...].T
    for g in range(2):
        cols = slice(g * 256, (g + 1) * 256)
        mixed[:, cols] = (hil[:, cols].astype(F32) + dot(context, w[g, :, 768:])).astype(BF)
    mixed_copy = pltpu.make_async_copy(mixed, mixed_hbm, sems.at[1])
    mixed_copy.start()
    rows = hil[...].astype(F32)
    centred = rows - jnp.mean(rows, axis=-1, keepdims=True)
    inv_scale = lax.rsqrt(jnp.mean(centred * centred, axis=-1, keepdims=True) + EPS)
    xhat = centred * inv_scale
    ngrad = dot_t(qkv_grad[:, :768], w[0, :, :768]) + dot_t(qkv_grad[:, 768:], w[1, :, :768])
    cent = ngrad - jnp.mean(ngrad, axis=-1, keepdims=True)
    cent = cent - xhat * jnp.mean(ngrad * xhat, axis=-1, keepdims=True)
    gout_copy.wait()
    hgrad = (gout[...].astype(F32) + inv_scale * cent).astype(BF)
    leave = departures(digits_ref[...])
    for c in range(0, 4, 2):
        out = dot(leave, hgrad[:, c * LANES : (c + 2) * LANES]).astype(BF)
        back[:, :, c * LANES : (c + 2) * LANES] = out.reshape(SHARDS, CAP, 2 * LANES)
    mixed_copy.wait()


def pair_kernel(keep_ref, theirs_ref, *out_refs):
    for k in range(4):
        out_refs[k][...] = (keep_ref[k].astype(F32) + theirs_ref[k].astype(F32)).astype(BF)


def total_kernel(factor, terms_ref, out_ref):
    total = terms_ref[0].astype(F32)
    for i in range(1, 64):
        total = total + terms_ref[i].astype(F32)
    out_ref[...] = jnp.broadcast_to((total * factor).astype(BF)[None], out_ref.shape)


def columns_kernel(blocks_ref, qkv_ref, out_ref):
    for y in range(8):
        for core in range(2):
            first = y // 2 * WIDTH + core * 256 + y % 2 * LANES
            block = blocks_ref[2 * y + core].astype(F32)
            if first < 3 * WIDTH:
                qkv_ref[:, first : first + LANES] = block
            else:
                out_ref[:, first - 3 * WIDTH : first - 3 * WIDTH + LANES] = block


def unpack_kernel(slot_ref, back_ref, out_ref):
    slot = slot_ref[0:1, :]
    row = iota((LANES, POINTS), 0)
    digits = jnp.where(row == 0, slot // 32, jnp.where(row == 1, slot % 32, 0))
    eye = onehot(iota((POINTS, POINTS), 0) == iota((POINTS, POINTS), 1))
    cols = dot_t(eye, digits.astype(F32).astype(BF))
    slot_col = (cols[:, 0:1] * 32.0 + cols[:, 1:2]).astype(jnp.int32)
    take = onehot(iota((POINTS, SLOTS), 1) == slot_col)
    for c in range(0, 4, 2):
        cols = slice(c * LANES, (c + 2) * LANES)
        got = back_ref[:, :, cols].reshape(SLOTS, 2 * LANES)
        out_ref[:, cols] = dot(take, got).astype(BF)


VMEM = pl.BlockSpec(memory_space=pltpu.VMEM)
SMEM = pl.BlockSpec(memory_space=pltpu.SMEM)
ANY = pl.BlockSpec(memory_space=pl.ANY)
HBM = pl.BlockSpec(memory_space=pltpu.HBM)


def params(mib):
    return pltpu.CompilerParams(vmem_limit_bytes=mib * 1024 * 1024)


def exchange(array, axes):
    return lax.all_to_all(array, axes, split_axis=0, concat_axis=0, tiled=True)


def cost(flops, size):
    return pl.CostEstimate(flops=flops, bytes_accessed=size, transcendentals=0)


def shift(array, axis, size, by):
    return lax.ppermute(array, axis, [(i, (i + by) % size) for i in range(size)])


def local(feats, hilbert_pos, w_qkv, w_out, grad_out):
    core, x = lax.axis_index("core"), lax.axis_index("x")
    at = jnp.stack([core, x]).astype(jnp.int32)
    pieces = [w_qkv[:, :WIDTH], w_qkv[:, WIDTH : 2 * WIDTH], w_qkv[:, 2 * WIDTH :], w_out]
    by_z = jnp.concatenate(
        [jnp.where(core == 0, piece[:, :256], piece[:, 256:]) for piece in pieces], axis=1
    )[None]
    by_z = exchange(jnp.broadcast_to(by_z, (8, 16, W_COLS)), "z").reshape(128, W_COLS)
    send, slot = pl.pallas_call(
        pack_kernel,
        out_shape=(
            jax.ShapeDtypeStruct((SHARDS, SEND_ROWS, LANES), BF),
            jax.ShapeDtypeStruct((8, POINTS), jnp.int32),
        ),
        in_specs=[VMEM, VMEM],
        out_specs=(VMEM, VMEM),
        compiler_params=params(12),
        cost_estimate=cost(10**9, 4 << 20),
        name="pack",
    )(hilbert_pos, feats[0])
    recv = exchange(send, SEQ)
    mine = [by_z] + [shift(by_z, "x", 4, k) for k in X_SHIFTS[1:]]
    other = shift(jnp.stack(mine), "core", 2, 1)
    wgrad = jax.ShapeDtypeStruct((4, 8, LANES, LANES), BF)
    hilbert, normed, digits = pl.pallas_call(
        arrive_kernel,
        out_shape=(
            jax.ShapeDtypeStruct((POINTS, WIDTH), BF),
            jax.ShapeDtypeStruct((POINTS, WIDTH), BF),
            jax.ShapeDtypeStruct((SHARDS, LANES), BF),
        ),
        in_specs=[VMEM],
        out_specs=(VMEM,) * 3,
        compiler_params=params(12),
        cost_estimate=cost(2 * 10**9, 4 << 20),
        name="arrive",
    )(recv)
    keep, give, weights, context_t, qkv_grad = pl.pallas_call(
        block_kernel,
        out_shape=(
            wgrad,
            wgrad,
            jax.ShapeDtypeStruct((2, WIDTH, W_COLS), BF),
            jax.ShapeDtypeStruct((WIDTH, POINTS), BF),
            jax.ShapeDtypeStruct((POINTS, 3 * WIDTH), BF),
        ),
        in_specs=[SMEM] + [VMEM] * 6 + [HBM],
        out_specs=(VMEM,) * 5,
        scratch_shapes=[
            pltpu.VMEM((POINTS, WIDTH), BF),
            pltpu.VMEM((WIDTH, POINTS), BF),
            pltpu.VMEM((POINTS, 3 * WIDTH), BF),
            pltpu.VMEM((POINTS, WIDTH), BF),
            pltpu.VMEM((2, 2, 8 * PATCH, PATCH), F32),
            pltpu.SemaphoreType.DMA((9,)),
        ],
        compiler_params=params(24),
        cost_estimate=cost(10**10, 8 << 20),
        name="block",
    )(at, normed, *mine, other, grad_out[0])
    mixed, back = pl.pallas_call(
        finish_kernel,
        out_shape=(
            jax.ShapeDtypeStruct((POINTS, WIDTH), BF),
            jax.ShapeDtypeStruct((SHARDS, CAP, WIDTH), BF),
        ),
        in_specs=[VMEM] * 5 + [HBM],
        out_specs=(ANY, VMEM),
        scratch_shapes=[
            pltpu.VMEM((POINTS, WIDTH), BF),
            pltpu.VMEM((POINTS, WIDTH), BF),
            pltpu.SemaphoreType.DMA((2,)),
        ],
        compiler_params=params(12),
        cost_estimate=cost(4 * 10**9, 8 << 20),
        name="finish",
    )(hilbert, digits, weights, context_t, qkv_grad, grad_out[0])
    theirs = shift(give, "core", 2, 1)
    pair = pl.pallas_call(
        pair_kernel,
        out_shape=(jax.ShapeDtypeStruct((8, LANES, LANES), BF),) * 4,
        in_specs=[VMEM, VMEM],
        out_specs=(VMEM,) * 4,
        compiler_params=params(12),
        cost_estimate=cost(10**6, 3 << 20),
        name="pair",
    )(keep, theirs)
    *pair, back = lax.optimization_barrier((*pair, back))
    returned = exchange(back, SEQ)
    by_x = [pair[0]] + [shift(pair[k], "x", 4, k) for k in (2, 3, 1)]
    *by_x, returned = lax.optimization_barrier((*by_x, returned))
    share = sum(term.astype(F32) for term in by_x).astype(BF)
    by_seq = exchange(share.reshape(64, WIDTH // SHARDS, LANES), ("y", "z"))
    factor = 1.0 / math.sqrt(16 * POINTS * SHARDS)
    total = pl.pallas_call(
        functools.partial(total_kernel, factor),
        out_shape=jax.ShapeDtypeStruct((16, WIDTH // SHARDS, LANES), BF),
        in_specs=[VMEM],
        out_specs=VMEM,
        compiler_params=params(16),
        cost_estimate=cost(10**6, 1 << 18),
        name="total",
    )(by_seq)
    whole = exchange(total, BATCH)
    qkv_wgrad, out_wgrad = pl.pallas_call(
        columns_kernel,
        out_shape=(
            jax.ShapeDtypeStruct((WIDTH // SHARDS, 3 * WIDTH), F32),
            jax.ShapeDtypeStruct((WIDTH // SHARDS, WIDTH), F32),
        ),
        in_specs=[VMEM],
        out_specs=(VMEM, VMEM),
        compiler_params=params(12),
        cost_estimate=cost(10**6, 1 << 18),
        name="columns",
    )(whole)
    feat_grad = pl.pallas_call(
        unpack_kernel,
        out_shape=jax.ShapeDtypeStruct((POINTS, WIDTH), BF),
        in_specs=[VMEM, VMEM],
        out_specs=VMEM,
        compiler_params=params(12),
        cost_estimate=cost(10**9, 4 << 20),
        name="unpack",
    )(slot, returned)
    return (mixed[None], feat_grad[None], qkv_wgrad, out_wgrad)


def solution(mesh):
    mesh = Mesh(mesh.devices.reshape(4, 8, 8, 2), ("x", "z", "y", "core"))
    rows = P(BATCH, SEQ, None)
    return jax.shard_map(
        local,
        mesh=mesh,
        in_specs=(rows, P(BATCH, SEQ), P(SEQ, None), P(SEQ, None), rows),
        out_specs=(rows, rows, P(SEQ, None), P(SEQ, None)),
        check_vma=False,
    )
```
